32 devices in a mesh: grp: 8 (over z, x), sub: 4 (over y, core).
Axes of the slice: x: 2, y: 2, z: 4, core: 2. Of those that a mesh axis runs over, the one named last changes fastest.
Arguments:
- field: float32 [128, 2, 16, 256], P(('grp', 'sub')), may hold values from -6 to 6
- source: float32 [128, 2, 16, 256], P(('grp', 'sub')), may hold values from -6 to 6
- patch_of_slot: int32 [128], P(('grp', 'sub')), may hold values from -1 to 11, as said below
- neighbour: int32 [128, 6], P(('grp', 'sub')), may hold values from -1 to 15, as said below
- wave_index: int32 [128], P(('grp', 'sub')), may hold values from 0 to 15
- wave_table: float32 [16], replicated, may hold values from 0.02 to 0.2
Outputs:
- corrected: float32 [128, 2, 16, 256], P(('grp', 'sub'))
The draws below stay inside these ranges and needn't reach their ends.
Inputs may be any that keep to these rules, and one draw needn't show every extreme that they name: `patch_of_slot`: in each slab every patch 0 to 11 is held by exactly one slot; each device holds 2 to 4 patches in its first slots, the rest -1; in every slab some device holds 4 and some 2. `neighbour`: consistent with patch_of_slot and the slab grid: -1 exactly for empty slots, for faces on the grid's boundary.
All inputs are finite; a program needn't handle non-finite values.
Results may differ from the reference program's by a relative error of at most 0.0003.
Values sent between devices are 32-bit elements; how exact they have to be, the bound alone decides.
A program may use at most 64 MiB of HBM per device.

```python
import math
import jax
import jax.numpy as jnp
from jax import lax

C = 16
P_DEV = 4
PZ = 4
NK = 16
CITER = 3
PY = 3
PPS = 12
GS = 16
SLOTS = 128
N_GRP = 8
N_SUB = 4


def group_layout(group_key):
    key_delta, key_pick, key_sign, key_order = jax.random.split(group_key, 4)
    pair_count = N_SUB // 2
    shift_delta = jax.random.randint(key_delta, (pair_count,), -1, 2)
    picked_pair = jax.random.randint(key_pick, (), 0, pair_count)
    signed_step = jax.random.randint(key_sign, (), 0, 2) * 2 - 1
    shift_delta = jnp.where(jnp.arange(pair_count) == picked_pair, signed_step, shift_delta)
    slot_counts = jnp.stack([3 + shift_delta, 3 - shift_delta], 1).reshape(N_SUB)
    slot_starts = jnp.cumsum(slot_counts) - slot_counts
    patch_order = jax.random.permutation(key_order, PPS)
    slot_position = jnp.arange(P_DEV)
    slot_index = slot_starts[:, None] + slot_position[None, :]
    live_slots = slot_position[None, :] < slot_counts[:, None]
    chosen_patch = patch_order[jnp.clip(slot_index, 0, PPS - 1)]
    return jnp.where(live_slots, chosen_patch, -1).reshape(GS).astype(jnp.int32)


def arrangement(key):
    base_key = jax.random.fold_in(key, 11)
    group_keys = jax.random.split(base_key, N_GRP)
    return jax.vmap(group_layout)(group_keys)


def draw_patch_of_slot(key, part):
    return arrangement(key).reshape(SLOTS)


def draw_neighbour(key, part):
    patches = arrangement(key)
    live_slots = patches >= 0
    target = jnp.where(live_slots, patches, PPS)
    slot_numbers = jnp.broadcast_to(jnp.arange(GS, dtype=jnp.int32), patches.shape)
    group_rows = jnp.arange(N_GRP)[:, None]
    inverse = jnp.zeros((N_GRP, PPS + 1), jnp.int32).at[group_rows, target].set(slot_numbers)[:, :PPS]
    safe_patch = jnp.where(live_slots, patches, 0)
    row_y = safe_patch // PZ
    col_z = safe_patch % PZ

    def lookup(group_index, patch_index, allowed):
        group_safe = jnp.clip(group_index, 0, N_GRP - 1)
        found = inverse[group_safe, jnp.clip(patch_index, 0, PPS - 1)]
        return jnp.where(allowed & live_slots, found, -1)
    group_full = jnp.broadcast_to(group_rows, patches.shape)
    lower_x = lookup(group_full - 1, safe_patch, group_full > 0)
    upper_x = lookup(group_full + 1, safe_patch, group_full < N_GRP - 1)
    lower_y = lookup(group_full, safe_patch - PZ, row_y > 0)
    upper_y = lookup(group_full, safe_patch + PZ, row_y < PY - 1)
    lower_z = lookup(group_full, safe_patch - 1, col_z > 0)
    upper_z = lookup(group_full, safe_patch + 1, col_z < PZ - 1)
    links = jnp.stack([lower_x, upper_x, lower_y, upper_y, lower_z, upper_z], -1)
    return links.reshape(SLOTS, 6).astype(jnp.int32)


def with_ends(values, own_key, smallest, high):
    index_at = [jax.random.randint(jax.random.fold_in(own_key, axis), (), 0, length) for axis, length in enumerate(values.shape)]
    main_axis = values.shape.index(max(values.shape))
    beside = index_at[:main_axis] + [(index_at[main_axis] + 1) % values.shape[main_axis]] + index_at[main_axis + 1:]
    return values.at[tuple(index_at)].set(smallest).at[tuple(beside)].set(high)


def block_scale(stream_key, shape, cuts, least, high):
    gain, own = 1.0, jax.random.fold_in(stream_key, 6)
    for position, parts in cuts:
        steps = jnp.exp(jax.random.uniform(jax.random.fold_in(own, position), (parts,), jnp.float32, least / len(cuts), high / len(cuts)))
        gain = gain * jnp.repeat(steps, shape[position] // parts).reshape([-1 if axis == position else 1 for axis in range(len(shape))])
    return gain


def gaussian(stream_key, extent, scale, bound, cuts=(), kind=jnp.bfloat16):
    loudness = block_scale(stream_key, extent, cuts, -0.22, 0.18) if cuts else 1.0
    drawn = jax.random.normal(stream_key, extent, jnp.float32) * scale * loudness
    return jnp.minimum(jnp.maximum(drawn, -bound), bound).astype(kind)


def setup_inputs(seed: int = 0) -> dict:
    key_of = jax.random.split(jax.random.key(seed), 7)
    return {
        "field": gaussian(key_of[0], (SLOTS, 2, C, C * C), 1.0, 6.0, ((0, 32),), jnp.float32),
        "source": gaussian(key_of[1], (SLOTS, 2, C, C * C), 1.0, 6.0, ((0, 32),), jnp.float32),
        "patch_of_slot": draw_patch_of_slot(jax.random.fold_in(key_of[6], 71), 0),
        "neighbour": draw_neighbour(jax.random.fold_in(key_of[6], 71), 0),
        "wave_index": with_ends(jax.random.randint(key_of[4], (SLOTS,), 0, NK), jax.random.fold_in(key_of[4], 1), 0, NK - 1).astype(jnp.int32),
        "wave_table": jnp.clip(jnp.exp(jax.random.uniform(key_of[5], (NK,), jnp.float32, math.log(0.02), math.log(0.2))), 0.02, 0.2),
    }


omega_fine = 0.7
omega_coarse = 0.6
shift_imag = 0.5


def faces_of(cubes):
    slot_count = cubes.shape[0]
    edge = cubes.shape[2]
    layers = [cubes[:, :, 0], cubes[:, :, -1], cubes[:, :, :, 0], cubes[:, :, :, -1], cubes[:, :, :, :, 0], cubes[:, :, :, :, -1]]
    return jnp.stack([layer.reshape(slot_count, 2, edge * edge) for layer in layers], 1)


def neighbour_sum(cubes, ghosts):
    slot_count = cubes.shape[0]
    edge = cubes.shape[2]
    ghost_sheets = ghosts.reshape(slot_count, 6, 2, edge, edge)
    total = jnp.concatenate([ghost_sheets[:, 0][:, :, None], cubes[:, :, :-1]], 2)
    total = total + jnp.concatenate([cubes[:, :, 1:], ghost_sheets[:, 1][:, :, None]], 2)
    total = total + jnp.concatenate([ghost_sheets[:, 2][:, :, :, None], cubes[:, :, :, :-1]], 3)
    total = total + jnp.concatenate([cubes[:, :, :, 1:], ghost_sheets[:, 3][:, :, :, None]], 3)
    total = total + jnp.concatenate([ghost_sheets[:, 4][..., None], cubes[..., :-1]], 4)
    total = total + jnp.concatenate([cubes[..., 1:], ghost_sheets[:, 5][..., None]], 4)
    return total


def residual_of(cubes, rights, ghosts, wave_sq):
    beside_all = neighbour_sum(cubes, ghosts)
    scale = wave_sq[:, None, None, None]
    real_part = cubes[:, 0]
    imag_part = cubes[:, 1]
    apply_real = 6.0 * real_part - beside_all[:, 0] - scale * (real_part - shift_imag * imag_part)
    apply_imag = 6.0 * imag_part - beside_all[:, 1] - scale * (imag_part + shift_imag * real_part)
    return jnp.stack([rights[:, 0] - apply_real, rights[:, 1] - apply_imag], 1)


def divide_diag(values, real_diag, imag_diag, channel_axis):
    denom = real_diag * real_diag + imag_diag * imag_diag
    first = jnp.take(values, 0, axis=channel_axis)
    second = jnp.take(values, 1, axis=channel_axis)
    out_real = (first * real_diag - second * imag_diag) / denom
    out_imag = (first * imag_diag + second * real_diag) / denom
    return jnp.stack([out_real, out_imag], channel_axis)


def smooth_step(cubes, resid, wave_sq):
    scale = wave_sq[:, None, None, None]
    step_value = divide_diag(resid, 6.0 - scale, shift_imag * scale, 1)
    return cubes + omega_fine * step_value


def restrict(resid):
    slot_count = resid.shape[0]
    edge = resid.shape[2]
    small = edge // 4
    blocks = resid.reshape(slot_count, 2, small, 4, small, 4, small, 4)
    return jnp.mean(blocks, axis=(3, 5, 7)).reshape(slot_count, 2 * small * small * small)


def coarse_residual(padded_x, coarse_rhs, coarse_wave):
    current = padded_x[:, 1:-1]
    beside_all = padded_x[:, :-2] + padded_x[:, 2:]
    ypad = jnp.pad(current, ((0, 0), (0, 0), (1, 1), (0, 0)))
    beside_all = beside_all + ypad[:, :, :-2] + ypad[:, :, 2:]
    zpad = jnp.pad(current, ((0, 0), (0, 0), (0, 0), (1, 1)))
    beside_all = beside_all + zpad[..., :-2] + zpad[..., 2:]
    real_part = current[0]
    imag_part = current[1]
    apply_real = (6.0 * real_part - beside_all[0]) / 16.0 - coarse_wave * (real_part - shift_imag * imag_part)
    apply_imag = (6.0 * imag_part - beside_all[1]) / 16.0 - coarse_wave * (imag_part + shift_imag * real_part)
    return jnp.stack([coarse_rhs[0] - apply_real, coarse_rhs[1] - apply_imag], 0)


def coarse_divide(values, coarse_wave):
    return divide_diag(values, 6.0 / 16.0 - coarse_wave, shift_imag * coarse_wave, 0)


def all_ghosts(cubes_all, links):
    groups = cubes_all.shape[0]
    per_group = cubes_all.shape[1]
    edge = cubes_all.shape[3]
    faces = faces_of(cubes_all.reshape((groups * per_group,) + cubes_all.shape[2:])).reshape(groups, per_group, 6, 2, edge * edge)
    blank = jnp.zeros_like(faces[:1, :, 0])
    lower = jnp.concatenate([blank, faces[:-1, :, 1]], 0)
    upper = jnp.concatenate([faces[1:, :, 0], blank], 0)
    candidate = jnp.concatenate([lower[:, :, None], upper[:, :, None], faces[:, :, 3:4], faces[:, :, 2:3], faces[:, :, 5:6], faces[:, :, 4:5]], 2)
    safe_links = jnp.maximum(links, 0)
    picked = candidate[jnp.arange(groups)[:, None, None], safe_links, jnp.arange(6)[None, None, :]]
    return jnp.where((links >= 0)[..., None, None], picked, 0.0)


def reference(field, source, patch_of_slot, neighbour, wave_index, wave_table):
    groups = N_GRP
    per_group = N_SUB * P_DEV
    edge = C
    small = edge // 4
    rows_y = PY
    patch_total = PPS
    cubes = field.reshape(groups, per_group, 2, edge, edge, edge)
    rights = source.reshape(groups, per_group, 2, edge, edge, edge)
    links = neighbour.reshape(groups, per_group, 6)
    wave_sq = wave_table[wave_index].reshape(groups, per_group)
    patch_ids = patch_of_slot.reshape(groups, per_group)

    def sweep_group(items):
        cube_g, right_g, ghost_g, wave_g = items
        return smooth_step(cube_g, residual_of(cube_g, right_g, ghost_g, wave_g), wave_g)

    for sweep_index in range(2):
        ghosts = all_ghosts(cubes, links)
        cubes = lax.map(sweep_group, (cubes, rights, ghosts, wave_sq))
    ghosts = all_ghosts(cubes, links)

    def restrict_group(items):
        cube_g, right_g, ghost_g, wave_g = items
        return restrict(residual_of(cube_g, right_g, ghost_g, wave_g))

    coarse_rows = lax.map(restrict_group, (cubes, rights, ghosts, wave_sq))

    def slab_group(items):
        rows_g, wave_g, ids_g = items
        selector = (ids_g[None, :] == jnp.arange(patch_total)[:, None]).astype(jnp.float32)
        placed = jnp.dot(selector, rows_g, precision=lax.Precision.HIGHEST)
        placed_wave = jnp.dot(selector, wave_g[:, None], precision=lax.Precision.HIGHEST)[:, 0]
        slab = placed.reshape(rows_y, PZ, 2, small, small, small).transpose(2, 3, 0, 4, 1, 5).reshape(2, small, rows_y * small, PZ * small)
        wave_grid = jnp.repeat(jnp.repeat(placed_wave.reshape(rows_y, PZ), small, 0), small, 1)
        return slab, wave_grid

    slabs, wave_grids = lax.map(slab_group, (coarse_rows, wave_sq, patch_ids))
    coarse_rhs = slabs.transpose(1, 0, 2, 3, 4).reshape(2, groups * small, rows_y * small, PZ * small)
    coarse_wave = jnp.repeat(wave_grids, small, 0)
    correction = omega_coarse * coarse_divide(coarse_rhs, coarse_wave)
    for sweep_index in range(CITER - 1):
        padded = jnp.pad(correction, ((0, 0), (1, 1), (0, 0), (0, 0)))
        correction = correction + omega_coarse * coarse_divide(coarse_residual(padded, coarse_rhs, coarse_wave), coarse_wave)
    patch_blocks = correction.reshape(2, groups, small, rows_y, small, PZ, small).transpose(1, 3, 5, 0, 2, 4, 6).reshape(groups, patch_total, 2, small, small, small)

    def prolong_group(items):
        cube_g, blocks_g, ids_g = items
        mine = blocks_g[jnp.maximum(ids_g, 0)]
        count = cube_g.shape[0]
        grown = jnp.broadcast_to(mine[:, :, :, None, :, None, :, None], (count, 2, small, 4, small, 4, small, 4)).reshape(count, 2, edge, edge, edge)
        return jnp.where((ids_g >= 0)[:, None, None, None, None], cube_g + grown, 0.0)

    result = lax.map(prolong_group, (cubes, patch_blocks, patch_ids))
    return result.reshape(groups * per_group, 2, edge, edge * edge)
```

```python
import functools

import jax
import jax.numpy as jnp
from jax import lax
from jax.experimental import pallas as pl
from jax.experimental.pallas import tpu as pltpu
from jax.sharding import PartitionSpec as P

PZ = 4
CITER = 3
ROUNDS = 3

omega_fine = 0.7
omega_coarse = 0.6
shift_imag = 0.5

F32 = jnp.float32
BF16 = jnp.bfloat16
MESH = pl.DeviceIdType.MESH


def iota(shape, axis):
    return lax.broadcasted_iota(jnp.int32, shape, axis)


def terms_of(values, count):
    terms = []
    for _ in range(count - 1):
        term = values.astype(BF16)
        terms.append(term)
        values = values - term.astype(F32)
    terms.append(values.astype(BF16))
    return terms


def times_selector(values, selector, count=2):
    rows = values.shape[0]
    stacked = jnp.concatenate(terms_of(values, count), 0)
    product = jnp.dot(stacked, selector, preferred_element_type=F32)
    total = product[:rows]
    for term in range(1, count):
        total = total + product[term * rows : (term + 1) * rows]
    return total


def face_cells(shape, lane_axis, opposite):
    lane = iota(shape, lane_axis)
    face = lane >> 5
    if opposite:
        face = face ^ 1
    place = lane & 15
    cell = jnp.where(
        face < 2,
        place + jnp.where(face == 1, 240, 0),
        place * 16 + jnp.where(face == 3, 15, 0),
    )
    return (lane >> 4) & 1, cell


def pack_matrix():
    shape = (512, 128)
    part, cell = face_cells(shape, 1, False)
    return (iota(shape, 0) == part * 256 + cell).astype(F32).astype(BF16)


def unpack_matrix():
    shape = (128, 512)
    part, cell = face_cells(shape, 0, True)
    return (iota(shape, 1) == part * 256 + cell).astype(F32).astype(BF16)


def block_match(fine, lane):
    same_part = (fine >> 8) == (lane >> 6)
    same_y = ((fine >> 6) & 3) == ((lane >> 2) & 3)
    same_z = ((fine >> 2) & 3) == (lane & 3)
    return (same_part & same_y & same_z).astype(F32).astype(BF16)


def kernel(
    n_grp,
    n_sub,
    patch_ref,
    link_ref,
    index_ref,
    table_ref,
    field_ref,
    source_ref,
    out_ref,
    faces_0,
    faces_1,
    faces_2,
    below_0,
    below_1,
    below_2,
    above_0,
    above_1,
    above_2,
    sheets,
    meta,
    rows,
    placed_e,
    slab_send,
    slab_recv,
    low_send,
    low_recv,
    high_send,
    high_recv,
):
    faces = (faces_0, faces_1, faces_2)
    below = (below_0, below_1, below_2)
    above = (above_0, above_1, above_2)
    slots = field_ref.shape[0]
    fine_rows = slots * 16
    patch_total = 3 * n_sub
    rows_y = patch_total // PZ
    patch_rows = -(-patch_total // 8) * 8
    g = lax.axis_index("grp")
    s = lax.axis_index("sub")
    has_low = g > 0
    has_high = g < n_grp - 1

    def beside(step):
        return lax.rem(s + step, n_sub)

    def before(step):
        return lax.rem(s + n_sub - step, n_sub)

    barrier = pltpu.get_barrier_semaphore()
    for step in range(1, n_sub):
        pl.semaphore_signal(barrier, inc=1, device_id=(g, beside(step)), device_id_type=MESH)

    @pl.when(has_low)
    def _():
        for step in range(n_sub):
            pl.semaphore_signal(
                barrier, inc=1, device_id=(g - 1, beside(step)), device_id_type=MESH
            )

    @pl.when(has_high)
    def _():
        for step in range(n_sub):
            pl.semaphore_signal(
                barrier, inc=1, device_id=(g + 1, beside(step)), device_id_type=MESH
            )

    def slab_copy(ref_of, stage, step, owner):
        ref = ref_of(owner)
        return pltpu.make_async_remote_copy(
            src_ref=ref,
            dst_ref=ref,
            send_sem=slab_send.at[stage, step],
            recv_sem=slab_recv.at[stage, step],
            device_id=(g, beside(step)),
            device_id_type=MESH,
        )

    def low_copy(src, dst, stage, step):
        return pltpu.make_async_remote_copy(
            src_ref=src,
            dst_ref=dst,
            send_sem=low_send.at[stage, step],
            recv_sem=high_recv.at[stage, step],
            device_id=(g - 1, beside(step)),
            device_id_type=MESH,
        )

    def high_copy(src, dst, stage, step):
        return pltpu.make_async_remote_copy(
            src_ref=src,
            dst_ref=dst,
            send_sem=high_send.at[stage, step],
            recv_sem=low_recv.at[stage, step],
            device_id=(g + 1, beside(step)),
            device_id_type=MESH,
        )

    def send(stage, slab_of, low_src, low_of, high_src, high_of):
        @pl.when(has_high)
        def _():
            for step in range(n_sub):
                high_copy(high_src, low_of(s), stage, step).start()

        @pl.when(has_low)
        def _():
            for step in range(n_sub):
                low_copy(low_src, high_of(s), stage, step).start()

        for step in range(1, n_sub):
            slab_copy(slab_of, stage, step, s).start()

    def receive(stage, slab_of, low_src, low_of, high_src, high_of):
        for step in range(1, n_sub):
            slab_copy(slab_of, stage, step, before(step)).wait_recv()

        @pl.when(has_low)
        def _():
            for step in range(n_sub):
                high_copy(high_src, low_of(before(step)), stage, step).wait_recv()

        @pl.when(has_high)
        def _():
            for step in range(n_sub):
                low_copy(low_src, high_of(before(step)), stage, step).wait_recv()

    def sent(stage, slab_of, low_src, low_of, high_src, high_of):
        for step in range(1, n_sub):
            slab_copy(slab_of, stage, step, s).wait_send()

        @pl.when(has_high)
        def _():
            for step in range(n_sub):
                high_copy(high_src, low_of(s), stage, step).wait_send()

        @pl.when(has_low)
        def _():
            for step in range(n_sub):
                low_copy(low_src, high_of(s), stage, step).wait_send()

    def face_exchange(stage):
        return (
            stage,
            lambda owner: faces[stage].at[pl.ds(owner * slots, slots)],
            sheets.at[stage, 0],
            lambda owner: below[stage].at[owner],
            sheets.at[stage, 1],
            lambda owner: above[stage].at[owner],
        )

    def row_exchange(stage, ref):
        mine = ref.at[1, s]
        return (
            stage,
            lambda owner: ref.at[1, owner],
            mine,
            lambda owner: ref.at[0, owner],
            mine,
            lambda owner: ref.at[2, owner],
        )

    meta_exchange = row_exchange(ROUNDS, meta)
    coarse_exchange = row_exchange(ROUNDS + 1, rows)

    @pl.when(jnp.logical_not(has_low))
    def _():
        for layers in below:
            layers[...] = jnp.zeros_like(layers)
        meta[0] = jnp.zeros_like(meta[0])
        rows[0] = jnp.zeros_like(rows[0])

    @pl.when(jnp.logical_not(has_high))
    def _():
        for layers in above:
            layers[...] = jnp.zeros_like(layers)
        meta[2] = jnp.zeros_like(meta[2])
        rows[2] = jnp.zeros_like(rows[2])

    wave_of = [table_ref[index_ref[slot]] for slot in range(slots)]
    patch_of = [patch_ref[slot] for slot in range(slots)]

    row8 = iota((8, 128), 0)
    meta_rows = jnp.zeros((8, 128), F32)
    for slot in range(slots):
        meta_rows = jnp.where(row8 == slot, wave_of[slot], meta_rows)
        meta_rows = jnp.where(
            row8 == slots + slot, (patch_of[slot] + 1).astype(F32), meta_rows
        )
    meta[1, s] = meta_rows

    def joined(ref, part):
        return jnp.concatenate([ref[slot, part] for slot in range(slots)], 0)

    real = joined(field_ref, 0)
    imag = joined(field_ref, 1)

    pack = pack_matrix()

    def put_faces(stage, real, imag):
        packed = times_selector(jnp.concatenate([real, imag], 1), pack)
        for slot in range(slots):
            faces[stage][s * slots + slot] = packed[slot * 16 : slot * 16 + 16]
        for side, edge_row in ((0, 0), (1, 15)):
            lines = []
            for half in range(2):
                for slot in range(slots):
                    for values in (real, imag):
                        row = slot * 16 + edge_row
                        lines.append(values[row : row + 1, half * 128 : half * 128 + 128])
            sheets[stage, side] = jnp.concatenate(lines, 0)

    put_faces(0, real, imag)

    greeted = n_sub - 1 + n_sub * (has_low.astype(jnp.int32) + has_high.astype(jnp.int32))
    pl.semaphore_wait(barrier, greeted)

    send(*face_exchange(0))
    send(*meta_exchange)

    source_real = joined(source_ref, 0)
    source_imag = joined(source_ref, 1)
    unpack = unpack_matrix()
    wave = jnp.concatenate([jnp.full((16, 256), wave_of[slot], F32) for slot in range(slots)], 0)
    real_diag = 6.0 - wave
    imag_diag = shift_imag * wave
    scale = omega_fine / (real_diag * real_diag + imag_diag * imag_diag)
    step_real = real_diag * scale
    step_imag = imag_diag * scale

    cell = iota((fine_rows, 256), 1)
    fine_i = iota((fine_rows, 256), 0) & 15
    y_low = cell < 16
    y_high = cell >= 240
    z_low = (cell & 15) == 0
    z_high = (cell & 15) == 15
    x_low = fine_i == 0
    x_high = fine_i == 15

    def inner_sum(values):
        total = jnp.where(y_low, 0.0, pltpu.roll(values, 16, 1))
        total = total + jnp.where(y_high, 0.0, pltpu.roll(values, 240, 1))
        total = total + jnp.where(z_low, 0.0, pltpu.roll(values, 1, 1))
        total = total + jnp.where(z_high, 0.0, pltpu.roll(values, 255, 1))
        total = total + jnp.where(x_low, 0.0, pltpu.roll(values, 1, 0))
        return total + jnp.where(x_high, 0.0, pltpu.roll(values, fine_rows - 1, 0))

    def local_part(real, imag):
        out_real = (
            source_real
            + inner_sum(real)
            - (6.0 * real - wave * (real - shift_imag * imag))
        )
        out_imag = (
            source_imag
            + inner_sum(imag)
            - (6.0 * imag - wave * (imag + shift_imag * real))
        )
        return out_real, out_imag

    links = [[link_ref[slot * 6 + face] for face in range(6)] for slot in range(slots)]
    safe = [[jnp.maximum(link, 0) for link in line] for line in links]
    valid = [[(link >= 0).astype(F32) for link in line] for line in links]
    packed_lane = iota((16, 128), 1) >> 5
    row16 = iota((16, 256), 0)

    def add_ghosts(stage, out_real, out_imag):
        blocks = []
        for slot in range(slots):
            got = [
                faces[stage][safe[slot][face]] * valid[slot][face] for face in range(2, 6)
            ]
            blocks.append(
                jnp.where(
                    packed_lane == 1,
                    got[0],
                    jnp.where(
                        packed_lane == 0,
                        got[1],
                        jnp.where(packed_lane == 3, got[2], got[3]),
                    ),
                )
            )
        spread = times_selector(jnp.concatenate(blocks, 0), unpack)
        result = []
        for part, own in ((0, out_real), (1, out_imag)):
            layers = []
            for slot in range(slots):
                layer = jnp.zeros((16, 256), F32)
                for face, ref, at in ((0, below, 0), (1, above, 15)):
                    link = safe[slot][face]
                    owner = link >> 2
                    first = (link & 3) * 2 + part
                    line = jnp.concatenate(
                        [
                            ref[stage][owner, pl.ds(first, 1), :],
                            ref[stage][owner, pl.ds(first + 8, 1), :],
                        ],
                        1,
                    )
                    layer = jnp.where(row16 == at, line * valid[slot][face], layer)
                layers.append(layer)
            ghosts = jnp.concatenate(layers, 0) + spread[:, part * 256 : part * 256 + 256]
            result.append(own + ghosts)
        return result

    for stage in range(2):
        resid = local_part(real, imag)
        receive(*face_exchange(stage))
        resid_real, resid_imag = add_ghosts(stage, *resid)
        real, imag = (
            real + (resid_real * step_real - resid_imag * step_imag),
            imag + (resid_real * step_imag + resid_imag * step_real),
        )
        put_faces(stage + 1, real, imag)
        send(*face_exchange(stage + 1))

    resid = local_part(real, imag)
    receive(*meta_exchange)
    gathered = n_sub * 8
    meta_row = iota((gathered, 128), 0)
    meta_lane = iota((gathered, 128), 1)
    selectors = []
    coarse = []
    lane = iota((patch_rows, 128), 1)
    patch = iota((patch_rows, 128), 0)
    sign = jnp.where(lane < 64, -1.0, 1.0)

    def placed_of(selector, values):
        terms = jnp.concatenate(terms_of(values, 3), 1)
        product = jnp.dot(selector, terms, preferred_element_type=F32)
        return product[:, :128] + product[:, 128:256] + product[:, 256:]

    for slab in range(3):
        known = meta[slab].reshape(gathered, 128)
        names = pltpu.roll(known, gathered - slots, 0)
        chosen = ((meta_row & 7) < slots) & (names == (meta_lane + 1).astype(F32))
        selector = chosen.astype(F32).T[:patch_rows].astype(BF16)
        selectors.append(selector)
        coarse_wave = placed_of(selector, known)
        diag = 6.0 / 16.0 - coarse_wave
        side = shift_imag * coarse_wave
        factor = omega_coarse / (diag * diag + side * side)
        coarse.append((coarse_wave, diag * factor, side * factor * sign))

    lane512 = iota((512, 128), 1)
    restrict = block_match(iota((512, 128), 0), lane512)
    grow = block_match(iota((128, 512), 1), iota((128, 512), 0))
    fine_lane = iota((fine_rows, 128), 1)
    same_x = ((iota((fine_rows, 128), 0) & 15) >> 2) == ((fine_lane >> 4) & 3)

    receive(*face_exchange(2))
    resid_real, resid_imag = add_ghosts(2, *resid)
    sums = times_selector(jnp.concatenate([resid_real, resid_imag], 1), restrict)
    sums = jnp.where(same_x, sums, 0.0) * (1.0 / 64.0)
    lines = [
        jnp.sum(sums[slot * 16 : slot * 16 + 16], axis=0, keepdims=True) for slot in range(slots)
    ]
    lines.append(jnp.zeros((8 - slots, 128), F32))
    rows[1, s] = jnp.concatenate(lines, 0)
    send(*coarse_exchange)

    lane_x = (lane >> 4) & 3
    lane_y = (lane >> 2) & 3
    lane_z = lane & 3
    patch_y = patch >> 2
    patch_z = patch & 3
    y_first = patch_y == 0
    y_last = patch_y >= rows_y - 1
    z_first = patch_z == 0
    z_last = patch_z == PZ - 1

    def turned(values, shift):
        return pltpu.roll(values, shift % 128, 1)

    def moved(values, shift):
        return pltpu.roll(values, shift % patch_rows, 0)

    def across(values, shift, outside):
        return jnp.where(outside, 0.0, moved(values, shift))

    def coarse_sum(lower, values, upper):
        x_down = turned(values, 16)
        x_up = turned(values, -16)
        edge = jnp.zeros_like(values) if lower is None else turned(lower, -48)
        total = jnp.where(lane_x == 0, edge, x_down)
        edge = jnp.zeros_like(values) if upper is None else turned(upper, 48)
        total = total + jnp.where(lane_x == 3, edge, x_up)
        total = total + jnp.where(
            lane_y == 0, turned(across(values, PZ, y_first), -12), turned(values, 4)
        )
        total = total + jnp.where(
            lane_y == 3, turned(across(values, -PZ, y_last), 12), turned(values, -4)
        )
        total = total + jnp.where(
            lane_z == 0, turned(across(values, 1, z_first), -3), turned(values, 1)
        )
        return total + jnp.where(
            lane_z == 3, turned(across(values, -1, z_last), 3), turned(values, -1)
        )

    def coarse_step(slab, values):
        _, near, cross = coarse[slab]
        return values * near + turned(values, 64) * cross

    receive(*coarse_exchange)
    right = [
        placed_of(selectors[slab], rows[slab].reshape(gathered, 128)) for slab in range(3)
    ]
    there = [has_low.astype(F32), None, has_high.astype(F32)]

    def kept(slab, values):
        return values if there[slab] is None else values * there[slab]

    errors = [kept(slab, coarse_step(slab, right[slab])) for slab in range(3)]
    for sweep in range(CITER - 1):
        following = list(errors)
        for slab in (0, 1, 2) if sweep < CITER - 2 else (1,):
            values = errors[slab]
            lower = errors[slab - 1] if slab > 0 else None
            upper = errors[slab + 1] if slab < 2 else None
            coarse_wave = coarse[slab][0]
            applied = (6.0 * values - coarse_sum(lower, values, upper)) * (1.0 / 16.0)
            applied = applied - coarse_wave * (
                values + shift_imag * sign * turned(values, 64)
            )
            following[slab] = kept(
                slab, values + coarse_step(slab, right[slab] - applied)
            )
        errors = following

    placed_e[...] = errors[1]
    grown = []
    for slot in range(slots):
        line = placed_e[pl.ds(jnp.maximum(patch_of[slot], 0), 1), :]
        grown.append(jnp.broadcast_to(line, (16, 128)))
    grown = jnp.where(same_x, jnp.concatenate(grown, 0), 0.0)
    grown = times_selector(grown, grow)
    for slot in range(slots):
        live = patch_of[slot] >= 0
        span = slice(slot * 16, slot * 16 + 16)
        out_ref[slot, 0] = jnp.where(live, real[span] + grown[span, :256], 0.0)
        out_ref[slot, 1] = jnp.where(live, imag[span] + grown[span, 256:], 0.0)

    for stage in range(ROUNDS):
        sent(*face_exchange(stage))
    sent(*meta_exchange)
    sent(*coarse_exchange)


def body(n_grp, n_sub, field, source, patch_of_slot, neighbour, wave_index, wave_table):
    slots = field.shape[0]
    patch_rows = -(-3 * n_sub // 8) * 8
    stages = ROUNDS + 2
    smem = pl.BlockSpec(memory_space=pltpu.SMEM)
    vmem = pl.BlockSpec(memory_space=pltpu.VMEM)
    dma = pltpu.SemaphoreType.DMA((stages, n_sub))
    return pl.pallas_call(
        functools.partial(kernel, n_grp, n_sub),
        out_shape=jax.ShapeDtypeStruct(field.shape, F32),
        in_specs=[smem] * 4 + [vmem] * 2,
        out_specs=vmem,
        scratch_shapes=[pltpu.VMEM((n_sub * slots, 16, 128), F32)] * ROUNDS
        + [pltpu.VMEM((n_sub, 4 * slots, 128), F32)] * (2 * ROUNDS)
        + [
            pltpu.VMEM((ROUNDS, 2, 4 * slots, 128), F32),
            pltpu.VMEM((3, n_sub, 8, 128), F32),
            pltpu.VMEM((3, n_sub, 8, 128), F32),
            pltpu.VMEM((patch_rows, 128), F32),
        ]
        + [dma] * 6,
        compiler_params=pltpu.CompilerParams(
            collective_id=0, has_side_effects=True, vmem_limit_bytes=24 * 1024 * 1024
        ),
    )(
        patch_of_slot,
        neighbour.reshape(-1),
        wave_index,
        wave_table,
        field,
        source,
    )


def solution(mesh):
    return jax.shard_map(
        functools.partial(body, mesh.shape["grp"], mesh.shape["sub"]),
        mesh=mesh,
        in_specs=(
            P(("grp", "sub"), None, None, None),
            P(("grp", "sub"), None, None, None),
            P(("grp", "sub")),
            P(("grp", "sub"), None),
            P(("grp", "sub")),
            P(),
        ),
        out_specs=P(("grp", "sub"), None, None, None),
        check_vma=False,
    )
```

```python
import functools

import jax
import jax.numpy as jnp
from jax import lax
from jax.experimental import pallas as pl
from jax.experimental.pallas import tpu as pltpu
from jax.sharding import PartitionSpec as P

PZ = 4
CITER = 3
ROUNDS = 3

omega_fine = 0.7
omega_coarse = 0.6
shift_imag = 0.5

F32 = jnp.float32
BF16 = jnp.bfloat16
MESH = pl.DeviceIdType.MESH


def iota(shape, axis):
    return lax.broadcasted_iota(jnp.int32, shape, axis)


def terms_of(values, count):
    terms = []
    for _ in range(count - 1):
        term = values.astype(BF16)
        terms.append(term)
        values = values - term.astype(F32)
    terms.append(values.astype(BF16))
    return terms


def times_selector(values, selector, count=2):
    rows = values.shape[0]
    stacked = jnp.concatenate(terms_of(values, count), 0)
    product = jnp.dot(stacked, selector, preferred_element_type=F32)
    total = product[:rows]
    for term in range(1, count):
        total = total + product[term * rows : (term + 1) * rows]
    return total


def face_cells(shape, lane_axis, opposite):
    lane = iota(shape, lane_axis)
    face = lane >> 5
    if opposite:
        face = face ^ 1
    place = lane & 15
    cell = jnp.where(
        face < 2,
        place + jnp.where(face == 1, 240, 0),
        place * 16 + jnp.where(face == 3, 15, 0),
    )
    return (lane >> 4) & 1, cell


def pack_matrix():
    shape = (512, 128)
    part, cell = face_cells(shape, 1, False)
    return (iota(shape, 0) == part * 256 + cell).astype(F32).astype(BF16)


def unpack_matrix():
    shape = (128, 512)
    part, cell = face_cells(shape, 0, True)
    return (iota(shape, 1) == part * 256 + cell).astype(F32).astype(BF16)


def block_match(fine, lane):
    same_part = (fine >> 8) == (lane >> 6)
    same_y = ((fine >> 6) & 3) == ((lane >> 2) & 3)
    same_z = ((fine >> 2) & 3) == (lane & 3)
    return (same_part & same_y & same_z).astype(F32).astype(BF16)


def kernel(
    n_grp,
    n_sub,
    patch_ref,
    link_ref,
    index_ref,
    table_ref,
    field_in,
    source_in,
    out_ref,
    field_ref,
    source_ref,
    input_sem,
    faces_0,
    faces_1,
    faces_2,
    below_0,
    below_1,
    below_2,
    above_0,
    above_1,
    above_2,
    sheets,
    meta,
    rows,
    placed_e,
    slab_send,
    slab_recv,
    low_send,
    low_recv,
    high_send,
    high_recv,
):
    faces = (faces_0, faces_1, faces_2)
    below = (below_0, below_1, below_2)
    above = (above_0, above_1, above_2)
    slots = field_ref.shape[0]
    fine_rows = slots * 16
    patch_total = 3 * n_sub
    rows_y = patch_total // PZ
    patch_rows = -(-patch_total // 8) * 8
    g = lax.axis_index("grp")
    s = lax.axis_index("sub")
    has_low = g > 0
    has_high = g < n_grp - 1

    def beside(step):
        return lax.rem(s + step, n_sub)

    def before(step):
        return lax.rem(s + n_sub - step, n_sub)

    field_copy = pltpu.make_async_copy(field_in, field_ref, input_sem.at[0])
    source_copy = pltpu.make_async_copy(source_in, source_ref, input_sem.at[1])
    field_copy.start()
    source_copy.start()

    barrier = pltpu.get_barrier_semaphore()
    for step in range(1, n_sub):
        pl.semaphore_signal(barrier, inc=1, device_id=(g, beside(step)), device_id_type=MESH)

    @pl.when(has_low)
    def _():
        for step in range(n_sub):
            pl.semaphore_signal(
                barrier, inc=1, device_id=(g - 1, beside(step)), device_id_type=MESH
            )

    @pl.when(has_high)
    def _():
        for step in range(n_sub):
            pl.semaphore_signal(
                barrier, inc=1, device_id=(g + 1, beside(step)), device_id_type=MESH
            )

    def slab_copy(ref_of, stage, step, owner):
        ref = ref_of(owner)
        return pltpu.make_async_remote_copy(
            src_ref=ref,
            dst_ref=ref,
            send_sem=slab_send.at[stage, step],
            recv_sem=slab_recv.at[stage, step],
            device_id=(g, beside(step)),
            device_id_type=MESH,
        )

    def low_copy(src, dst, stage, step):
        return pltpu.make_async_remote_copy(
            src_ref=src,
            dst_ref=dst,
            send_sem=low_send.at[stage, step],
            recv_sem=high_recv.at[stage, step],
            device_id=(g - 1, beside(step)),
            device_id_type=MESH,
        )

    def high_copy(src, dst, stage, step):
        return pltpu.make_async_remote_copy(
            src_ref=src,
            dst_ref=dst,
            send_sem=high_send.at[stage, step],
            recv_sem=low_recv.at[stage, step],
            device_id=(g + 1, beside(step)),
            device_id_type=MESH,
        )

    def send_slab(stage, slab_of, *_):
        for step in range(1, n_sub):
            slab_copy(slab_of, stage, step, s).start()

    def send_across(stage, slab_of, low_src, low_of, high_src, high_of):
        @pl.when(has_high)
        def _():
            for step in range(n_sub):
                high_copy(high_src, low_of(s), stage, step).start()

        @pl.when(has_low)
        def _():
            for step in range(n_sub):
                low_copy(low_src, high_of(s), stage, step).start()

    def receive_slab(stage, slab_of, *_):
        for step in range(1, n_sub):
            slab_copy(slab_of, stage, step, before(step)).wait_recv()

    def receive_across(stage, slab_of, low_src, low_of, high_src, high_of):
        @pl.when(has_low)
        def _():
            for step in range(n_sub):
                high_copy(high_src, low_of(before(step)), stage, step).wait_recv()

        @pl.when(has_high)
        def _():
            for step in range(n_sub):
                low_copy(low_src, high_of(before(step)), stage, step).wait_recv()

    def sent(stage, slab_of, low_src, low_of, high_src, high_of):
        for step in range(1, n_sub):
            slab_copy(slab_of, stage, step, s).wait_send()

        @pl.when(has_high)
        def _():
            for step in range(n_sub):
                high_copy(high_src, low_of(s), stage, step).wait_send()

        @pl.when(has_low)
        def _():
            for step in range(n_sub):
                low_copy(low_src, high_of(s), stage, step).wait_send()

    def face_exchange(stage):
        return (
            stage,
            lambda owner: faces[stage].at[pl.ds(owner * slots, slots)],
            sheets.at[stage, 0],
            lambda owner: below[stage].at[owner],
            sheets.at[stage, 1],
            lambda owner: above[stage].at[owner],
        )

    def row_exchange(stage, ref):
        mine = ref.at[1, s]
        return (
            stage,
            lambda owner: ref.at[1, owner],
            mine,
            lambda owner: ref.at[0, owner],
            mine,
            lambda owner: ref.at[2, owner],
        )

    meta_exchange = row_exchange(ROUNDS, meta)
    coarse_exchange = row_exchange(ROUNDS + 1, rows)

    @pl.when(jnp.logical_not(has_low))
    def _():
        for layers in below:
            layers[...] = jnp.zeros_like(layers)
        meta[0] = jnp.zeros_like(meta[0])
        rows[0] = jnp.zeros_like(rows[0])

    @pl.when(jnp.logical_not(has_high))
    def _():
        for layers in above:
            layers[...] = jnp.zeros_like(layers)
        meta[2] = jnp.zeros_like(meta[2])
        rows[2] = jnp.zeros_like(rows[2])

    wave_of = [table_ref[index_ref[slot]] for slot in range(slots)]
    patch_of = [patch_ref[slot] for slot in range(slots)]

    row8 = iota((8, 128), 0)
    meta_rows = jnp.zeros((8, 128), F32)
    for slot in range(slots):
        meta_rows = jnp.where(row8 == slot, wave_of[slot], meta_rows)
        meta_rows = jnp.where(
            row8 == slots + slot, (patch_of[slot] + 1).astype(F32), meta_rows
        )
    meta[1, s] = meta_rows

    def joined(ref, part):
        return jnp.concatenate([ref[slot, part] for slot in range(slots)], 0)

    pack = pack_matrix()
    field_copy.wait()
    real = joined(field_ref, 0)
    imag = joined(field_ref, 1)

    def put_sheets(stage, real, imag):
        for side, edge_row in ((0, 0), (1, 15)):
            lines = []
            for half in range(2):
                for slot in range(slots):
                    for values in (real, imag):
                        row = slot * 16 + edge_row
                        lines.append(values[row : row + 1, half * 128 : half * 128 + 128])
            sheets[stage, side] = jnp.concatenate(lines, 0)

    def put_faces(stage, real, imag):
        packed = times_selector(jnp.concatenate([real, imag], 1), pack)
        for slot in range(slots):
            faces[stage][s * slots + slot] = packed[slot * 16 : slot * 16 + 16]

    put_sheets(0, real, imag)
    put_faces(0, real, imag)

    greeted = n_sub - 1 + n_sub * (has_low.astype(jnp.int32) + has_high.astype(jnp.int32))
    pl.semaphore_wait(barrier, greeted)

    send_slab(*face_exchange(0))
    send_across(*face_exchange(0))
    send_slab(*meta_exchange)
    send_across(*meta_exchange)

    source_copy.wait()
    source_real = joined(source_ref, 0)
    source_imag = joined(source_ref, 1)
    unpack = unpack_matrix()
    wave = jnp.concatenate([jnp.full((16, 256), wave_of[slot], F32) for slot in range(slots)], 0)
    real_diag = 6.0 - wave
    imag_diag = shift_imag * wave
    scale = omega_fine / (real_diag * real_diag + imag_diag * imag_diag)
    step_real = real_diag * scale
    step_imag = imag_diag * scale

    cell = iota((fine_rows, 256), 1)
    fine_i = iota((fine_rows, 256), 0) & 15
    y_low = cell < 16
    y_high = cell >= 240
    z_low = (cell & 15) == 0
    z_high = (cell & 15) == 15
    x_low = fine_i == 0
    x_high = fine_i == 15

    def inner_sum(values):
        total = jnp.where(y_low, 0.0, pltpu.roll(values, 16, 1))
        total = total + jnp.where(y_high, 0.0, pltpu.roll(values, 240, 1))
        total = total + jnp.where(z_low, 0.0, pltpu.roll(values, 1, 1))
        total = total + jnp.where(z_high, 0.0, pltpu.roll(values, 255, 1))
        total = total + jnp.where(x_low, 0.0, pltpu.roll(values, 1, 0))
        return total + jnp.where(x_high, 0.0, pltpu.roll(values, fine_rows - 1, 0))

    def local_part(real, imag):
        out_real = (
            source_real
            + inner_sum(real)
            - (6.0 * real - wave * (real - shift_imag * imag))
        )
        out_imag = (
            source_imag
            + inner_sum(imag)
            - (6.0 * imag - wave * (imag + shift_imag * real))
        )
        return out_real, out_imag

    links = [[link_ref[slot, face] for face in range(6)] for slot in range(slots)]
    safe = [[jnp.maximum(link, 0) for link in line] for line in links]
    valid = [[(link >= 0).astype(F32) for link in line] for line in links]
    packed_lane = iota((16, 128), 1) >> 5
    row16 = iota((16, 256), 0)

    def add_ghosts(stage, out_real, out_imag):
        receive_slab(*face_exchange(stage))
        blocks = []
        for slot in range(slots):
            got = [
                faces[stage][safe[slot][face]] * valid[slot][face] for face in range(2, 6)
            ]
            blocks.append(
                jnp.where(
                    packed_lane == 1,
                    got[0],
                    jnp.where(
                        packed_lane == 0,
                        got[1],
                        jnp.where(packed_lane == 3, got[2], got[3]),
                    ),
                )
            )
        spread = times_selector(jnp.concatenate(blocks, 0), unpack)
        out_real = out_real + spread[:, :256]
        out_imag = out_imag + spread[:, 256:]
        receive_across(*face_exchange(stage))
        result = []
        for part, own in ((0, out_real), (1, out_imag)):
            layers = []
            for slot in range(slots):
                layer = jnp.zeros((16, 256), F32)
                for face, ref, at in ((0, below, 0), (1, above, 15)):
                    link = safe[slot][face]
                    owner = link >> 2
                    first = (link & 3) * 2 + part
                    line = jnp.concatenate(
                        [
                            ref[stage][owner, pl.ds(first, 1), :],
                            ref[stage][owner, pl.ds(first + 8, 1), :],
                        ],
                        1,
                    )
                    layer = jnp.where(row16 == at, line * valid[slot][face], layer)
                layers.append(layer)
            result.append(own + jnp.concatenate(layers, 0))
        return result

    for stage in range(2):
        resid = local_part(real, imag)
        resid_real, resid_imag = add_ghosts(stage, *resid)
        real, imag = (
            real + (resid_real * step_real - resid_imag * step_imag),
            imag + (resid_real * step_imag + resid_imag * step_real),
        )
        put_sheets(stage + 1, real, imag)
        send_across(*face_exchange(stage + 1))
        put_faces(stage + 1, real, imag)
        send_slab(*face_exchange(stage + 1))

    resid = local_part(real, imag)
    receive_slab(*meta_exchange)
    receive_across(*meta_exchange)
    gathered = n_sub * 8
    meta_row = iota((gathered, 128), 0)
    meta_lane = iota((gathered, 128), 1)
    selectors = []
    coarse = []
    lane = iota((patch_rows, 128), 1)
    patch = iota((patch_rows, 128), 0)
    sign = jnp.where(lane < 64, -1.0, 1.0)

    def placed_of(selector, values):
        terms = jnp.concatenate(terms_of(values, 3), 1)
        product = jnp.dot(selector, terms, preferred_element_type=F32)
        return product[:, :128] + product[:, 128:256] + product[:, 256:]

    for slab in range(3):
        known = meta[slab].reshape(gathered, 128)
        names = pltpu.roll(known, gathered - slots, 0)
        chosen = ((meta_row & 7) < slots) & (names == (meta_lane + 1).astype(F32))
        selector = chosen.astype(F32).T[:patch_rows].astype(BF16)
        selectors.append(selector)
        coarse_wave = placed_of(selector, known)
        diag = 6.0 / 16.0 - coarse_wave
        side = shift_imag * coarse_wave
        factor = omega_coarse / (diag * diag + side * side)
        coarse.append((coarse_wave, diag * factor, side * factor * sign))

    lane512 = iota((512, 128), 1)
    restrict = block_match(iota((512, 128), 0), lane512)
    grow = block_match(iota((128, 512), 1), iota((128, 512), 0))
    fine_lane = iota((fine_rows, 128), 1)
    same_x = ((iota((fine_rows, 128), 0) & 15) >> 2) == ((fine_lane >> 4) & 3)

    resid_real, resid_imag = add_ghosts(2, *resid)
    sums = times_selector(jnp.concatenate([resid_real, resid_imag], 1), restrict)
    sums = jnp.where(same_x, sums, 0.0) * (1.0 / 64.0)
    lines = [
        jnp.sum(sums[slot * 16 : slot * 16 + 16], axis=0, keepdims=True) for slot in range(slots)
    ]
    lines.append(jnp.zeros((8 - slots, 128), F32))
    rows[1, s] = jnp.concatenate(lines, 0)
    send_across(*coarse_exchange)
    send_slab(*coarse_exchange)

    lane_x = (lane >> 4) & 3
    lane_y = (lane >> 2) & 3
    lane_z = lane & 3
    patch_y = patch >> 2
    patch_z = patch & 3
    y_first = patch_y == 0
    y_last = patch_y >= rows_y - 1
    z_first = patch_z == 0
    z_last = patch_z == PZ - 1

    def turned(values, shift):
        return pltpu.roll(values, shift % 128, 1)

    def moved(values, shift):
        return pltpu.roll(values, shift % patch_rows, 0)

    def across(values, shift, outside):
        return jnp.where(outside, 0.0, moved(values, shift))

    def coarse_sum(lower, values, upper):
        x_down = turned(values, 16)
        x_up = turned(values, -16)
        edge = jnp.zeros_like(values) if lower is None else turned(lower, -48)
        total = jnp.where(lane_x == 0, edge, x_down)
        edge = jnp.zeros_like(values) if upper is None else turned(upper, 48)
        total = total + jnp.where(lane_x == 3, edge, x_up)
        total = total + jnp.where(
            lane_y == 0, turned(across(values, PZ, y_first), -12), turned(values, 4)
        )
        total = total + jnp.where(
            lane_y == 3, turned(across(values, -PZ, y_last), 12), turned(values, -4)
        )
        total = total + jnp.where(
            lane_z == 0, turned(across(values, 1, z_first), -3), turned(values, 1)
        )
        return total + jnp.where(
            lane_z == 3, turned(across(values, -1, z_last), 3), turned(values, -1)
        )

    def coarse_step(slab, values):
        _, near, cross = coarse[slab]
        return values * near + turned(values, 64) * cross

    receive_slab(*coarse_exchange)
    receive_across(*coarse_exchange)
    right = [
        placed_of(selectors[slab], rows[slab].reshape(gathered, 128)) for slab in range(3)
    ]
    there = [has_low.astype(F32), None, has_high.astype(F32)]

    def kept(slab, values):
        return values if there[slab] is None else values * there[slab]

    errors = [kept(slab, coarse_step(slab, right[slab])) for slab in range(3)]
    for sweep in range(CITER - 1):
        following = list(errors)
        for slab in (0, 1, 2) if sweep < CITER - 2 else (1,):
            values = errors[slab]
            lower = errors[slab - 1] if slab > 0 else None
            upper = errors[slab + 1] if slab < 2 else None
            coarse_wave = coarse[slab][0]
            applied = (6.0 * values - coarse_sum(lower, values, upper)) * (1.0 / 16.0)
            applied = applied - coarse_wave * (
                values + shift_imag * sign * turned(values, 64)
            )
            following[slab] = kept(
                slab, values + coarse_step(slab, right[slab] - applied)
            )
        errors = following

    placed_e[...] = errors[1]
    grown = []
    for slot in range(slots):
        line = placed_e[pl.ds(jnp.maximum(patch_of[slot], 0), 1), :]
        grown.append(jnp.broadcast_to(line, (16, 128)))
    grown = jnp.where(same_x, jnp.concatenate(grown, 0), 0.0)
    grown = times_selector(grown, grow)
    for slot in range(slots):
        live = patch_of[slot] >= 0
        span = slice(slot * 16, slot * 16 + 16)
        out_ref[slot, 0] = jnp.where(live, real[span] + grown[span, :256], 0.0)
        out_ref[slot, 1] = jnp.where(live, imag[span] + grown[span, 256:], 0.0)

    for stage in range(ROUNDS):
        sent(*face_exchange(stage))
    sent(*meta_exchange)
    sent(*coarse_exchange)


def body(n_grp, n_sub, field, source, patch_of_slot, neighbour, wave_index, wave_table):
    slots = field.shape[0]
    patch_rows = -(-3 * n_sub // 8) * 8
    stages = ROUNDS + 2
    smem = pl.BlockSpec(memory_space=pltpu.SMEM)
    vmem = pl.BlockSpec(memory_space=pltpu.VMEM)
    dma = pltpu.SemaphoreType.DMA((stages, n_sub))
    return pl.pallas_call(
        functools.partial(kernel, n_grp, n_sub),
        out_shape=jax.ShapeDtypeStruct(field.shape, F32),
        in_specs=[smem] * 4 + [pl.BlockSpec(memory_space=pltpu.HBM)] * 2,
        out_specs=vmem,
        scratch_shapes=[pltpu.VMEM(field.shape, F32)] * 2
        + [pltpu.SemaphoreType.DMA((2,))]
        + [pltpu.VMEM((n_sub * slots, 16, 128), F32)] * ROUNDS
        + [pltpu.VMEM((n_sub, 4 * slots, 128), F32)] * (2 * ROUNDS)
        + [
            pltpu.VMEM((ROUNDS, 2, 4 * slots, 128), F32),
            pltpu.VMEM((3, n_sub, 8, 128), F32),
            pltpu.VMEM((3, n_sub, 8, 128), F32),
            pltpu.VMEM((patch_rows, 128), F32),
        ]
        + [dma] * 6,
        compiler_params=pltpu.CompilerParams(
            collective_id=0, has_side_effects=True, vmem_limit_bytes=63 * 1024 * 1024
        ),
    )(
        patch_of_slot,
        neighbour,
        wave_index,
        wave_table,
        field,
        source,
    )


def solution(mesh):
    return jax.shard_map(
        functools.partial(body, mesh.shape["grp"], mesh.shape["sub"]),
        mesh=mesh,
        in_specs=(
            P(("grp", "sub"), None, None, None),
            P(("grp", "sub"), None, None, None),
            P(("grp", "sub")),
            P(("grp", "sub"), None),
            P(("grp", "sub")),
            P(),
        ),
        out_specs=P(("grp", "sub"), None, None, None),
        check_vma=False,
    )
```

```python
import functools

import jax
import jax.numpy as jnp
from jax import lax
from jax.experimental import pallas as pl
from jax.experimental.pallas import tpu as pltpu
from jax.sharding import PartitionSpec as P

PZ = 4
CITER = 3
ROUNDS = 3

omega_fine = 0.7
omega_coarse = 0.6
shift_imag = 0.5

F32 = jnp.float32
BF16 = jnp.bfloat16
MESH = pl.DeviceIdType.MESH


def iota(shape, axis):
    return lax.broadcasted_iota(jnp.int32, shape, axis)


def terms_of(values, count):
    terms = []
    for _ in range(count - 1):
        term = values.astype(BF16)
        terms.append(term)
        values = values - term.astype(F32)
    terms.append(values.astype(BF16))
    return terms


def times_selector(values, selector, count=2):
    rows = values.shape[0]
    stacked = jnp.concatenate(terms_of(values, count), 0)
    product = jnp.dot(stacked, selector, preferred_element_type=F32)
    total = product[:rows]
    for term in range(1, count):
        total = total + product[term * rows : (term + 1) * rows]
    return total


def face_cells(shape, lane_axis, opposite):
    lane = iota(shape, lane_axis)
    face = lane >> 5
    if opposite:
        face = face ^ 1
    place = lane & 15
    cell = jnp.where(
        face < 2,
        place + jnp.where(face == 1, 240, 0),
        place * 16 + jnp.where(face == 3, 15, 0),
    )
    return (lane >> 4) & 1, cell


def pack_matrix():
    shape = (512, 128)
    part, cell = face_cells(shape, 1, False)
    return (iota(shape, 0) == part * 256 + cell).astype(F32).astype(BF16)


def unpack_matrix():
    shape = (128, 512)
    part, cell = face_cells(shape, 0, True)
    return (iota(shape, 1) == part * 256 + cell).astype(F32).astype(BF16)


def block_match(fine, lane):
    same_part = (fine >> 8) == (lane >> 6)
    same_y = ((fine >> 6) & 3) == ((lane >> 2) & 3)
    same_z = ((fine >> 2) & 3) == (lane & 3)
    return (same_part & same_y & same_z).astype(F32).astype(BF16)


def kernel(
    n_grp,
    n_sub,
    patch_ref,
    link_ref,
    index_ref,
    table_ref,
    field_in,
    source_in,
    out_ref,
    field_ref,
    source_ref,
    input_sem,
    faces_0,
    faces_1,
    faces_2,
    below_0,
    below_1,
    below_2,
    above_0,
    above_1,
    above_2,
    sheets,
    meta,
    rows,
    placed_e,
    slab_send,
    slab_recv,
    low_send,
    low_recv,
    high_send,
    high_recv,
):
    faces = (faces_0, faces_1, faces_2)
    below = (below_0, below_1, below_2)
    above = (above_0, above_1, above_2)
    slots = field_ref.shape[0]
    fine_rows = slots * 16
    patch_total = 3 * n_sub
    rows_y = patch_total // PZ
    patch_rows = -(-patch_total // 8) * 8
    g = lax.axis_index("grp")
    s = lax.axis_index("sub")
    has_low = g > 0
    has_high = g < n_grp - 1

    def beside(step):
        return lax.rem(s + step, n_sub)

    def before(step):
        return lax.rem(s + n_sub - step, n_sub)

    field_copy = pltpu.make_async_copy(field_in, field_ref, input_sem.at[0])
    source_copy = pltpu.make_async_copy(source_in, source_ref, input_sem.at[1])
    field_copy.start()
    source_copy.start()

    barrier = pltpu.get_barrier_semaphore()
    for step in range(1, n_sub):
        pl.semaphore_signal(barrier, inc=1, device_id=(g, beside(step)), device_id_type=MESH)

    @pl.when(has_low)
    def _():
        for step in range(n_sub):
            pl.semaphore_signal(
                barrier, inc=1, device_id=(g - 1, beside(step)), device_id_type=MESH
            )

    @pl.when(has_high)
    def _():
        for step in range(n_sub):
            pl.semaphore_signal(
                barrier, inc=1, device_id=(g + 1, beside(step)), device_id_type=MESH
            )

    def slab_copy(ref_of, stage, step, owner):
        ref = ref_of(owner)
        return pltpu.make_async_remote_copy(
            src_ref=ref,
            dst_ref=ref,
            send_sem=slab_send.at[stage, step],
            recv_sem=slab_recv.at[stage, step],
            device_id=(g, beside(step)),
            device_id_type=MESH,
        )

    def low_copy(src, dst, stage, step):
        return pltpu.make_async_remote_copy(
            src_ref=src,
            dst_ref=dst,
            send_sem=low_send.at[stage, step],
            recv_sem=high_recv.at[stage, step],
            device_id=(g - 1, beside(step)),
            device_id_type=MESH,
        )

    def high_copy(src, dst, stage, step):
        return pltpu.make_async_remote_copy(
            src_ref=src,
            dst_ref=dst,
            send_sem=high_send.at[stage, step],
            recv_sem=low_recv.at[stage, step],
            device_id=(g + 1, beside(step)),
            device_id_type=MESH,
        )

    other = s + 1 - 2 * lax.rem(s, 2)

    def face_copy(stage, owner, to, sem):
        ref = faces[stage].at[pl.ds(owner * slots, slots)]
        return pltpu.make_async_remote_copy(
            src_ref=ref,
            dst_ref=ref,
            send_sem=slab_send.at[stage, sem],
            recv_sem=slab_recv.at[stage, sem],
            device_id=(g, to),
            device_id_type=MESH,
        )

    def send_faces(stage):
        for step in range(2, n_sub, 2):
            face_copy(stage, s, beside(step), step).start()
        face_copy(stage, s, other, 1).start()

    def forward_faces(stage):
        for step in range(2, n_sub, 2):
            face_copy(stage, before(step), other, step).wait_recv()
            face_copy(stage, before(step), other, step + 1).start()

    def receive_faces(stage):
        face_copy(stage, other, other, 1).wait_recv()
        for step in range(2, n_sub, 2):
            owner = lax.rem(other + n_sub - step, n_sub)
            face_copy(stage, owner, other, step + 1).wait_recv()

    def sent_faces(stage):
        for step in range(2, n_sub, 2):
            face_copy(stage, s, beside(step), step).wait_send()
            face_copy(stage, before(step), other, step + 1).wait_send()
        face_copy(stage, s, other, 1).wait_send()

    def send_slab(stage, slab_of, *_):
        for step in range(1, n_sub):
            slab_copy(slab_of, stage, step, s).start()

    def send_across(stage, slab_of, low_src, low_of, high_src, high_of):
        @pl.when(has_high)
        def _():
            for step in range(n_sub):
                high_copy(high_src, low_of(s), stage, step).start()

        @pl.when(has_low)
        def _():
            for step in range(n_sub):
                low_copy(low_src, high_of(s), stage, step).start()

    def receive_slab(stage, slab_of, *_):
        for step in range(1, n_sub):
            slab_copy(slab_of, stage, step, before(step)).wait_recv()

    def receive_across(stage, slab_of, low_src, low_of, high_src, high_of):
        @pl.when(has_low)
        def _():
            for step in range(n_sub):
                high_copy(high_src, low_of(before(step)), stage, step).wait_recv()

        @pl.when(has_high)
        def _():
            for step in range(n_sub):
                low_copy(low_src, high_of(before(step)), stage, step).wait_recv()

    def sent_slab(stage, slab_of, *_):
        for step in range(1, n_sub):
            slab_copy(slab_of, stage, step, s).wait_send()

    def sent_across(stage, slab_of, low_src, low_of, high_src, high_of):
        @pl.when(has_high)
        def _():
            for step in range(n_sub):
                high_copy(high_src, low_of(s), stage, step).wait_send()

        @pl.when(has_low)
        def _():
            for step in range(n_sub):
                low_copy(low_src, high_of(s), stage, step).wait_send()

    def face_exchange(stage):
        return (
            stage,
            None,
            sheets.at[stage, 0],
            lambda owner: below[stage].at[owner],
            sheets.at[stage, 1],
            lambda owner: above[stage].at[owner],
        )

    def row_exchange(stage, ref):
        mine = ref.at[1, s]
        return (
            stage,
            lambda owner: ref.at[1, owner],
            mine,
            lambda owner: ref.at[0, owner],
            mine,
            lambda owner: ref.at[2, owner],
        )

    meta_exchange = row_exchange(ROUNDS, meta)
    coarse_exchange = row_exchange(ROUNDS + 1, rows)

    @pl.when(jnp.logical_not(has_low))
    def _():
        for layers in below:
            layers[...] = jnp.zeros_like(layers)
        meta[0] = jnp.zeros_like(meta[0])
        rows[0] = jnp.zeros_like(rows[0])

    @pl.when(jnp.logical_not(has_high))
    def _():
        for layers in above:
            layers[...] = jnp.zeros_like(layers)
        meta[2] = jnp.zeros_like(meta[2])
        rows[2] = jnp.zeros_like(rows[2])

    wave_of = [table_ref[index_ref[slot]] for slot in range(slots)]
    patch_of = [patch_ref[slot] for slot in range(slots)]

    row8 = iota((8, 128), 0)
    meta_rows = jnp.zeros((8, 128), F32)
    for slot in range(slots):
        meta_rows = jnp.where(row8 == slot, wave_of[slot], meta_rows)
        meta_rows = jnp.where(
            row8 == slots + slot, (patch_of[slot] + 1).astype(F32), meta_rows
        )
    meta[1, s] = meta_rows

    def joined(ref, part):
        return jnp.concatenate([ref[slot, part] for slot in range(slots)], 0)

    pack = pack_matrix()
    field_copy.wait()
    real = joined(field_ref, 0)
    imag = joined(field_ref, 1)

    def put_sheets(stage, real, imag):
        for side, edge_row in ((0, 0), (1, 15)):
            lines = []
            for half in range(2):
                for slot in range(slots):
                    for values in (real, imag):
                        row = slot * 16 + edge_row
                        lines.append(values[row : row + 1, half * 128 : half * 128 + 128])
            sheets[stage, side] = jnp.concatenate(lines, 0)

    def put_faces(stage, real, imag):
        packed = times_selector(jnp.concatenate([real, imag], 1), pack)
        for slot in range(slots):
            faces[stage][s * slots + slot] = packed[slot * 16 : slot * 16 + 16]

    put_sheets(0, real, imag)
    put_faces(0, real, imag)

    greeted = n_sub - 1 + n_sub * (has_low.astype(jnp.int32) + has_high.astype(jnp.int32))
    pl.semaphore_wait(barrier, greeted)

    send_faces(0)
    send_across(*face_exchange(0))
    send_slab(*meta_exchange)
    send_across(*meta_exchange)

    source_copy.wait()
    source_real = joined(source_ref, 0)
    source_imag = joined(source_ref, 1)
    unpack = unpack_matrix()
    wave = jnp.concatenate([jnp.full((16, 256), wave_of[slot], F32) for slot in range(slots)], 0)
    real_diag = 6.0 - wave
    imag_diag = shift_imag * wave
    scale = omega_fine / (real_diag * real_diag + imag_diag * imag_diag)
    step_real = real_diag * scale
    step_imag = imag_diag * scale

    cell = iota((fine_rows, 256), 1)
    fine_i = iota((fine_rows, 256), 0) & 15
    y_low = cell < 16
    y_high = cell >= 240
    z_low = (cell & 15) == 0
    z_high = (cell & 15) == 15
    x_low = fine_i == 0
    x_high = fine_i == 15

    def inner_sum(values):
        total = jnp.where(y_low, 0.0, pltpu.roll(values, 16, 1))
        total = total + jnp.where(y_high, 0.0, pltpu.roll(values, 240, 1))
        total = total + jnp.where(z_low, 0.0, pltpu.roll(values, 1, 1))
        total = total + jnp.where(z_high, 0.0, pltpu.roll(values, 255, 1))
        total = total + jnp.where(x_low, 0.0, pltpu.roll(values, 1, 0))
        return total + jnp.where(x_high, 0.0, pltpu.roll(values, fine_rows - 1, 0))

    def local_part(real, imag):
        out_real = (
            source_real
            + inner_sum(real)
            - (6.0 * real - wave * (real - shift_imag * imag))
        )
        out_imag = (
            source_imag
            + inner_sum(imag)
            - (6.0 * imag - wave * (imag + shift_imag * real))
        )
        return out_real, out_imag

    links = [[link_ref[slot, face] for face in range(6)] for slot in range(slots)]
    safe = [[jnp.maximum(link, 0) for link in line] for line in links]
    valid = [[(link >= 0).astype(F32) for link in line] for line in links]
    packed_lane = iota((16, 128), 1) >> 5
    row16 = iota((16, 256), 0)

    def add_ghosts(stage, out_real, out_imag):
        receive_faces(stage)
        blocks = []
        for slot in range(slots):
            got = [
                faces[stage][safe[slot][face]] * valid[slot][face] for face in range(2, 6)
            ]
            blocks.append(
                jnp.where(
                    packed_lane == 1,
                    got[0],
                    jnp.where(
                        packed_lane == 0,
                        got[1],
                        jnp.where(packed_lane == 3, got[2], got[3]),
                    ),
                )
            )
        spread = times_selector(jnp.concatenate(blocks, 0), unpack)
        out_real = out_real + spread[:, :256]
        out_imag = out_imag + spread[:, 256:]
        receive_across(*face_exchange(stage))
        result = []
        for part, own in ((0, out_real), (1, out_imag)):
            layers = []
            for slot in range(slots):
                layer = jnp.zeros((16, 256), F32)
                for face, ref, at in ((0, below, 0), (1, above, 15)):
                    link = safe[slot][face]
                    owner = link >> 2
                    first = (link & 3) * 2 + part
                    line = jnp.concatenate(
                        [
                            ref[stage][owner, pl.ds(first, 1), :],
                            ref[stage][owner, pl.ds(first + 8, 1), :],
                        ],
                        1,
                    )
                    layer = jnp.where(row16 == at, line * valid[slot][face], layer)
                layers.append(layer)
            result.append(own + jnp.concatenate(layers, 0))
        return result

    for stage in range(2):
        resid = local_part(real, imag)
        forward_faces(stage)
        resid_real, resid_imag = add_ghosts(stage, *resid)
        real, imag = (
            real + (resid_real * step_real - resid_imag * step_imag),
            imag + (resid_real * step_imag + resid_imag * step_real),
        )
        put_sheets(stage + 1, real, imag)
        put_faces(stage + 1, real, imag)
        send_faces(stage + 1)
        send_across(*face_exchange(stage + 1))

    resid = local_part(real, imag)
    forward_faces(2)
    receive_slab(*meta_exchange)
    receive_across(*meta_exchange)
    gathered = n_sub * 8
    meta_row = iota((gathered, 128), 0)
    meta_lane = iota((gathered, 128), 1)
    selectors = []
    coarse = []
    lane = iota((patch_rows, 128), 1)
    patch = iota((patch_rows, 128), 0)
    sign = jnp.where(lane < 64, -1.0, 1.0)

    def placed_of(selector, values):
        terms = jnp.concatenate(terms_of(values, 3), 1)
        product = jnp.dot(selector, terms, preferred_element_type=F32)
        return product[:, :128] + product[:, 128:256] + product[:, 256:]

    for slab in range(3):
        known = meta[slab].reshape(gathered, 128)
        names = pltpu.roll(known, gathered - slots, 0)
        chosen = ((meta_row & 7) < slots) & (names == (meta_lane + 1).astype(F32))
        selector = chosen.astype(F32).T[:patch_rows].astype(BF16)
        selectors.append(selector)
        coarse_wave = placed_of(selector, known)
        diag = 6.0 / 16.0 - coarse_wave
        side = shift_imag * coarse_wave
        factor = omega_coarse / (diag * diag + side * side)
        coarse.append((coarse_wave, diag * factor, side * factor * sign))

    lane512 = iota((512, 128), 1)
    restrict = block_match(iota((512, 128), 0), lane512)
    grow = block_match(iota((128, 512), 1), iota((128, 512), 0))
    fine_lane = iota((fine_rows, 128), 1)
    same_x = ((iota((fine_rows, 128), 0) & 15) >> 2) == ((fine_lane >> 4) & 3)

    resid_real, resid_imag = add_ghosts(2, *resid)
    sums = times_selector(jnp.concatenate([resid_real, resid_imag], 1), restrict)
    sums = jnp.where(same_x, sums, 0.0) * (1.0 / 64.0)
    lines = [
        jnp.sum(sums[slot * 16 : slot * 16 + 16], axis=0, keepdims=True) for slot in range(slots)
    ]
    lines.append(jnp.zeros((8 - slots, 128), F32))
    rows[1, s] = jnp.concatenate(lines, 0)
    send_across(*coarse_exchange)
    send_slab(*coarse_exchange)

    lane_x = (lane >> 4) & 3
    lane_y = (lane >> 2) & 3
    lane_z = lane & 3
    patch_y = patch >> 2
    patch_z = patch & 3
    y_first = patch_y == 0
    y_last = patch_y >= rows_y - 1
    z_first = patch_z == 0
    z_last = patch_z == PZ - 1

    def turned(values, shift):
        return pltpu.roll(values, shift % 128, 1)

    def moved(values, shift):
        return pltpu.roll(values, shift % patch_rows, 0)

    def across(values, shift, outside):
        return jnp.where(outside, 0.0, moved(values, shift))

    def coarse_sum(lower, values, upper):
        x_down = turned(values, 16)
        x_up = turned(values, -16)
        edge = jnp.zeros_like(values) if lower is None else turned(lower, -48)
        total = jnp.where(lane_x == 0, edge, x_down)
        edge = jnp.zeros_like(values) if upper is None else turned(upper, 48)
        total = total + jnp.where(lane_x == 3, edge, x_up)
        total = total + jnp.where(
            lane_y == 0, turned(across(values, PZ, y_first), -12), turned(values, 4)
        )
        total = total + jnp.where(
            lane_y == 3, turned(across(values, -PZ, y_last), 12), turned(values, -4)
        )
        total = total + jnp.where(
            lane_z == 0, turned(across(values, 1, z_first), -3), turned(values, 1)
        )
        return total + jnp.where(
            lane_z == 3, turned(across(values, -1, z_last), 3), turned(values, -1)
        )

    def coarse_step(slab, values):
        _, near, cross = coarse[slab]
        return values * near + turned(values, 64) * cross

    receive_slab(*coarse_exchange)
    receive_across(*coarse_exchange)
    right = [
        placed_of(selectors[slab], rows[slab].reshape(gathered, 128)) for slab in range(3)
    ]
    there = [has_low.astype(F32), None, has_high.astype(F32)]

    def kept(slab, values):
        return values if there[slab] is None else values * there[slab]

    errors = [kept(slab, coarse_step(slab, right[slab])) for slab in range(3)]
    for sweep in range(CITER - 1):
        following = list(errors)
        for slab in (0, 1, 2) if sweep < CITER - 2 else (1,):
            values = errors[slab]
            lower = errors[slab - 1] if slab > 0 else None
            upper = errors[slab + 1] if slab < 2 else None
            coarse_wave = coarse[slab][0]
            applied = (6.0 * values - coarse_sum(lower, values, upper)) * (1.0 / 16.0)
            applied = applied - coarse_wave * (
                values + shift_imag * sign * turned(values, 64)
            )
            following[slab] = kept(
                slab, values + coarse_step(slab, right[slab] - applied)
            )
        errors = following

    placed_e[...] = errors[1]
    grown = []
    for slot in range(slots):
        line = placed_e[pl.ds(jnp.maximum(patch_of[slot], 0), 1), :]
        grown.append(jnp.broadcast_to(line, (16, 128)))
    grown = jnp.where(same_x, jnp.concatenate(grown, 0), 0.0)
    grown = times_selector(grown, grow)
    for slot in range(slots):
        live = patch_of[slot] >= 0
        span = slice(slot * 16, slot * 16 + 16)
        out_ref[slot, 0] = jnp.where(live, real[span] + grown[span, :256], 0.0)
        out_ref[slot, 1] = jnp.where(live, imag[span] + grown[span, 256:], 0.0)

    for stage in range(ROUNDS):
        sent_faces(stage)
        sent_across(*face_exchange(stage))
    for exchange in (meta_exchange, coarse_exchange):
        sent_slab(*exchange)
        sent_across(*exchange)


def body(n_grp, n_sub, field, source, patch_of_slot, neighbour, wave_index, wave_table):
    slots = field.shape[0]
    patch_rows = -(-3 * n_sub // 8) * 8
    stages = ROUNDS + 2
    smem = pl.BlockSpec(memory_space=pltpu.SMEM)
    vmem = pl.BlockSpec(memory_space=pltpu.VMEM)
    dma = pltpu.SemaphoreType.DMA((stages, n_sub))
    return pl.pallas_call(
        functools.partial(kernel, n_grp, n_sub),
        out_shape=jax.ShapeDtypeStruct(field.shape, F32),
        in_specs=[smem] * 4 + [pl.BlockSpec(memory_space=pltpu.HBM)] * 2,
        out_specs=vmem,
        scratch_shapes=[pltpu.VMEM(field.shape, F32)] * 2
        + [pltpu.SemaphoreType.DMA((2,))]
        + [pltpu.VMEM((n_sub * slots, 16, 128), F32)] * ROUNDS
        + [pltpu.VMEM((n_sub, 4 * slots, 128), F32)] * (2 * ROUNDS)
        + [
            pltpu.VMEM((ROUNDS, 2, 4 * slots, 128), F32),
            pltpu.VMEM((3, n_sub, 8, 128), F32),
            pltpu.VMEM((3, n_sub, 8, 128), F32),
            pltpu.VMEM((patch_rows, 128), F32),
        ]
        + [dma] * 6,
        compiler_params=pltpu.CompilerParams(
            collective_id=0, has_side_effects=True, vmem_limit_bytes=63 * 1024 * 1024
        ),
    )(
        patch_of_slot,
        neighbour,
        wave_index,
        wave_table,
        field,
        source,
    )


def solution(mesh):
    return jax.shard_map(
        functools.partial(body, mesh.shape["grp"], mesh.shape["sub"]),
        mesh=mesh,
        in_specs=(
            P(("grp", "sub"), None, None, None),
            P(("grp", "sub"), None, None, None),
            P(("grp", "sub")),
            P(("grp", "sub"), None),
            P(("grp", "sub")),
            P(),
        ),
        out_specs=P(("grp", "sub"), None, None, None),
        check_vma=False,
    )
```

```python
import functools

import jax
import jax.numpy as jnp
from jax import lax
from jax.experimental import pallas as pl
from jax.experimental.pallas import tpu as pltpu
from jax.sharding import PartitionSpec as P

PZ = 4
CITER = 3
ROUNDS = 3

omega_fine = 0.7
omega_coarse = 0.6
shift_imag = 0.5

F32 = jnp.float32
BF16 = jnp.bfloat16
MESH = pl.DeviceIdType.MESH


def iota(shape, axis):
    return lax.broadcasted_iota(jnp.int32, shape, axis)


def terms_of(values, count):
    terms = []
    for _ in range(count - 1):
        term = values.astype(BF16)
        terms.append(term)
        values = values - term.astype(F32)
    terms.append(values.astype(BF16))
    return terms


def times_selector(values, selector, count=2):
    rows = values.shape[0]
    stacked = jnp.concatenate(terms_of(values, count), 0)
    product = jnp.dot(stacked, selector, preferred_element_type=F32)
    total = product[:rows]
    for term in range(1, count):
        total = total + product[term * rows : (term + 1) * rows]
    return total


def face_cells(shape, lane_axis, opposite):
    lane = iota(shape, lane_axis)
    face = lane >> 5
    if opposite:
        face = face ^ 1
    place = lane & 15
    cell = jnp.where(
        face < 2,
        place + jnp.where(face == 1, 240, 0),
        place * 16 + jnp.where(face == 3, 15, 0),
    )
    return (lane >> 4) & 1, cell


def pack_matrix():
    shape = (512, 128)
    part, cell = face_cells(shape, 1, False)
    return (iota(shape, 0) == part * 256 + cell).astype(F32).astype(BF16)


def unpack_matrix():
    shape = (128, 512)
    part, cell = face_cells(shape, 0, True)
    return (iota(shape, 1) == part * 256 + cell).astype(F32).astype(BF16)


def block_match(fine, lane):
    same_part = (fine >> 8) == (lane >> 6)
    same_y = ((fine >> 6) & 3) == ((lane >> 2) & 3)
    same_z = ((fine >> 2) & 3) == (lane & 3)
    return (same_part & same_y & same_z).astype(F32).astype(BF16)


def kernel(
    n_grp,
    n_sub,
    patch_ref,
    link_ref,
    index_ref,
    table_ref,
    field_in,
    source_in,
    out_ref,
    field_ref,
    source_ref,
    input_sem,
    faces_0,
    faces_1,
    faces_2,
    below_0,
    below_1,
    below_2,
    above_0,
    above_1,
    above_2,
    sheets,
    meta,
    rows,
    placed_e,
    slab_send,
    slab_recv,
    low_send,
    low_recv,
    high_send,
    high_recv,
):
    faces = (faces_0, faces_1, faces_2)
    below = (below_0, below_1, below_2)
    above = (above_0, above_1, above_2)
    slots = field_ref.shape[0]
    fine_rows = slots * 16
    patch_total = 3 * n_sub
    rows_y = patch_total // PZ
    patch_rows = -(-patch_total // 8) * 8
    g = lax.axis_index("grp")
    s = lax.axis_index("sub")
    has_low = g > 0
    has_high = g < n_grp - 1

    def beside(step):
        return lax.rem(s + step, n_sub)

    def before(step):
        return lax.rem(s + n_sub - step, n_sub)

    field_copy = pltpu.make_async_copy(field_in, field_ref, input_sem.at[0])
    source_copy = pltpu.make_async_copy(source_in, source_ref, input_sem.at[1])
    field_copy.start()
    source_copy.start()

    barrier = pltpu.get_barrier_semaphore()
    for step in range(1, n_sub):
        pl.semaphore_signal(barrier, inc=1, device_id=(g, beside(step)), device_id_type=MESH)

    @pl.when(has_low)
    def _():
        for step in range(n_sub):
            pl.semaphore_signal(
                barrier, inc=1, device_id=(g - 1, beside(step)), device_id_type=MESH
            )

    @pl.when(has_high)
    def _():
        for step in range(n_sub):
            pl.semaphore_signal(
                barrier, inc=1, device_id=(g + 1, beside(step)), device_id_type=MESH
            )

    def slab_copy(ref_of, stage, step, owner):
        ref = ref_of(owner)
        return pltpu.make_async_remote_copy(
            src_ref=ref,
            dst_ref=ref,
            send_sem=slab_send.at[stage, step],
            recv_sem=slab_recv.at[stage, step],
            device_id=(g, beside(step)),
            device_id_type=MESH,
        )

    def low_copy(src, dst, stage, step):
        return pltpu.make_async_remote_copy(
            src_ref=src,
            dst_ref=dst,
            send_sem=low_send.at[stage, step],
            recv_sem=high_recv.at[stage, step],
            device_id=(g - 1, beside(step)),
            device_id_type=MESH,
        )

    def high_copy(src, dst, stage, step):
        return pltpu.make_async_remote_copy(
            src_ref=src,
            dst_ref=dst,
            send_sem=high_send.at[stage, step],
            recv_sem=low_recv.at[stage, step],
            device_id=(g + 1, beside(step)),
            device_id_type=MESH,
        )

    other = s + 1 - 2 * lax.rem(s, 2)

    def face_copy(stage, owner, to, sem):
        ref = faces[stage].at[pl.ds(owner * slots, slots)]
        return pltpu.make_async_remote_copy(
            src_ref=ref,
            dst_ref=ref,
            send_sem=slab_send.at[stage, sem],
            recv_sem=slab_recv.at[stage, sem],
            device_id=(g, to),
            device_id_type=MESH,
        )

    def send_faces(stage):
        for step in range(2, n_sub, 2):
            face_copy(stage, s, beside(step), step).start()
        face_copy(stage, s, other, 1).start()

    def forward_faces(stage):
        for step in range(2, n_sub, 2):
            face_copy(stage, before(step), other, step).wait_recv()
            face_copy(stage, before(step), other, step + 1).start()

    def receive_faces(stage):
        face_copy(stage, other, other, 1).wait_recv()
        for step in range(2, n_sub, 2):
            owner = lax.rem(other + n_sub - step, n_sub)
            face_copy(stage, owner, other, step + 1).wait_recv()

    def sent_faces(stage):
        for step in range(2, n_sub, 2):
            face_copy(stage, s, beside(step), step).wait_send()
            face_copy(stage, before(step), other, step + 1).wait_send()
        face_copy(stage, s, other, 1).wait_send()

    def send_slab(stage, slab_of, *_):
        for step in range(1, n_sub):
            slab_copy(slab_of, stage, step, s).start()

    def send_across(stage, slab_of, low_src, low_of, high_src, high_of):
        @pl.when(has_high)
        def _():
            for step in range(n_sub):
                high_copy(high_src, low_of(s), stage, step).start()

        @pl.when(has_low)
        def _():
            for step in range(n_sub):
                low_copy(low_src, high_of(s), stage, step).start()

    def receive_slab(stage, slab_of, *_):
        for step in range(1, n_sub):
            slab_copy(slab_of, stage, step, before(step)).wait_recv()

    def receive_across(stage, slab_of, low_src, low_of, high_src, high_of):
        @pl.when(has_low)
        def _():
            for step in range(n_sub):
                high_copy(high_src, low_of(before(step)), stage, step).wait_recv()

        @pl.when(has_high)
        def _():
            for step in range(n_sub):
                low_copy(low_src, high_of(before(step)), stage, step).wait_recv()

    def sent_slab(stage, slab_of, *_):
        for step in range(1, n_sub):
            slab_copy(slab_of, stage, step, s).wait_send()

    def sent_across(stage, slab_of, low_src, low_of, high_src, high_of):
        @pl.when(has_high)
        def _():
            for step in range(n_sub):
                high_copy(high_src, low_of(s), stage, step).wait_send()

        @pl.when(has_low)
        def _():
            for step in range(n_sub):
                low_copy(low_src, high_of(s), stage, step).wait_send()

    def face_exchange(stage):
        return (
            stage,
            None,
            sheets.at[stage, 0],
            lambda owner: below[stage].at[owner],
            sheets.at[stage, 1],
            lambda owner: above[stage].at[owner],
        )

    def row_exchange(stage, ref):
        mine = ref.at[1, s]
        return (
            stage,
            lambda owner: ref.at[1, owner],
            mine,
            lambda owner: ref.at[0, owner],
            mine,
            lambda owner: ref.at[2, owner],
        )

    meta_exchange = row_exchange(ROUNDS, meta)
    coarse_exchange = row_exchange(ROUNDS + 1, rows)

    @pl.when(jnp.logical_not(has_low))
    def _():
        for layers in below:
            layers[...] = jnp.zeros_like(layers)
        meta[0] = jnp.zeros_like(meta[0])
        rows[0] = jnp.zeros_like(rows[0])

    @pl.when(jnp.logical_not(has_high))
    def _():
        for layers in above:
            layers[...] = jnp.zeros_like(layers)
        meta[2] = jnp.zeros_like(meta[2])
        rows[2] = jnp.zeros_like(rows[2])

    wave_of = [table_ref[index_ref[slot]] for slot in range(slots)]
    patch_of = [patch_ref[slot] for slot in range(slots)]

    row8 = iota((8, 128), 0)
    meta_rows = jnp.zeros((8, 128), F32)
    for slot in range(slots):
        meta_rows = jnp.where(row8 == slot, wave_of[slot], meta_rows)
        meta_rows = jnp.where(
            row8 == slots + slot, (patch_of[slot] + 1).astype(F32), meta_rows
        )
    meta[1, s] = meta_rows

    def joined(ref, part):
        return jnp.concatenate([ref[slot, part] for slot in range(slots)], 0)

    pack = pack_matrix()
    field_copy.wait()
    real = joined(field_ref, 0)
    imag = joined(field_ref, 1)

    def put_sheets(stage, real, imag):
        for side, edge_row in ((0, 0), (1, 15)):
            lines = []
            for half in range(2):
                for slot in range(slots):
                    for values in (real, imag):
                        row = slot * 16 + edge_row
                        lines.append(values[row : row + 1, half * 128 : half * 128 + 128])
            sheets[stage, side] = jnp.concatenate(lines, 0)

    def put_faces(stage, real, imag):
        packed = times_selector(jnp.concatenate([real, imag], 1), pack)
        for slot in range(slots):
            faces[stage][s * slots + slot] = packed[slot * 16 : slot * 16 + 16]

    put_sheets(0, real, imag)
    put_faces(0, real, imag)

    greeted = n_sub - 1 + n_sub * (has_low.astype(jnp.int32) + has_high.astype(jnp.int32))
    pl.semaphore_wait(barrier, greeted)

    send_faces(0)
    send_across(*face_exchange(0))
    send_slab(*meta_exchange)
    send_across(*meta_exchange)

    source_copy.wait()
    source_real = joined(source_ref, 0)
    source_imag = joined(source_ref, 1)
    unpack = unpack_matrix()
    wave = jnp.concatenate([jnp.full((16, 256), wave_of[slot], F32) for slot in range(slots)], 0)
    real_diag = 6.0 - wave
    imag_diag = shift_imag * wave
    scale = omega_fine / (real_diag * real_diag + imag_diag * imag_diag)
    step_real = real_diag * scale
    step_imag = imag_diag * scale

    cell = iota((fine_rows, 256), 1)
    fine_i = iota((fine_rows, 256), 0) & 15
    y_low = cell < 16
    y_high = cell >= 240
    z_low = (cell & 15) == 0
    z_high = (cell & 15) == 15
    x_low = fine_i == 0
    x_high = fine_i == 15

    def inner_sum(values):
        total = jnp.where(y_low, 0.0, pltpu.roll(values, 16, 1))
        total = total + jnp.where(y_high, 0.0, pltpu.roll(values, 240, 1))
        total = total + jnp.where(z_low, 0.0, pltpu.roll(values, 1, 1))
        total = total + jnp.where(z_high, 0.0, pltpu.roll(values, 255, 1))
        total = total + jnp.where(x_low, 0.0, pltpu.roll(values, 1, 0))
        return total + jnp.where(x_high, 0.0, pltpu.roll(values, fine_rows - 1, 0))

    def local_part(real, imag):
        out_real = (
            source_real
            + inner_sum(real)
            - (6.0 * real - wave * (real - shift_imag * imag))
        )
        out_imag = (
            source_imag
            + inner_sum(imag)
            - (6.0 * imag - wave * (imag + shift_imag * real))
        )
        return out_real, out_imag

    links = [[link_ref[slot, face] for face in range(6)] for slot in range(slots)]
    safe = [[jnp.maximum(link, 0) for link in line] for line in links]
    valid = [[(link >= 0).astype(F32) for link in line] for line in links]
    packed_lane = iota((16, 128), 1) >> 5
    row16 = iota((16, 256), 0)

    def add_ghosts(stage, out_real, out_imag):
        receive_faces(stage)
        blocks = []
        for slot in range(slots):
            got = [
                faces[stage][safe[slot][face]] * valid[slot][face] for face in range(2, 6)
            ]
            blocks.append(
                jnp.where(
                    packed_lane == 1,
                    got[0],
                    jnp.where(
                        packed_lane == 0,
                        got[1],
                        jnp.where(packed_lane == 3, got[2], got[3]),
                    ),
                )
            )
        spread = times_selector(jnp.concatenate(blocks, 0), unpack)
        out_real = out_real + spread[:, :256]
        out_imag = out_imag + spread[:, 256:]
        receive_across(*face_exchange(stage))
        result = []
        for part, own in ((0, out_real), (1, out_imag)):
            layers = []
            for slot in range(slots):
                layer = jnp.zeros((16, 256), F32)
                for face, ref, at in ((0, below, 0), (1, above, 15)):
                    link = safe[slot][face]
                    owner = link >> 2
                    first = (link & 3) * 2 + part
                    line = jnp.concatenate(
                        [
                            ref[stage][owner, pl.ds(first, 1), :],
                            ref[stage][owner, pl.ds(first + 8, 1), :],
                        ],
                        1,
                    )
                    layer = jnp.where(row16 == at, line * valid[slot][face], layer)
                layers.append(layer)
            result.append(own + jnp.concatenate(layers, 0))
        return result

    for stage in range(2):
        resid = local_part(real, imag)
        forward_faces(stage)
        resid_real, resid_imag = add_ghosts(stage, *resid)
        real, imag = (
            real + (resid_real * step_real - resid_imag * step_imag),
            imag + (resid_real * step_imag + resid_imag * step_real),
        )
        put_sheets(stage + 1, real, imag)
        send_across(*face_exchange(stage + 1))
        put_faces(stage + 1, real, imag)
        send_faces(stage + 1)

    resid = local_part(real, imag)
    forward_faces(2)
    receive_slab(*meta_exchange)
    receive_across(*meta_exchange)
    gathered = n_sub * 8
    meta_row = iota((gathered, 128), 0)
    meta_lane = iota((gathered, 128), 1)
    selectors = []
    coarse = []
    lane = iota((patch_rows, 128), 1)
    patch = iota((patch_rows, 128), 0)
    sign = jnp.where(lane < 64, -1.0, 1.0)

    def placed_of(selector, values):
        terms = jnp.concatenate(terms_of(values, 3), 1)
        product = jnp.dot(selector, terms, preferred_element_type=F32)
        return product[:, :128] + product[:, 128:256] + product[:, 256:]

    for slab in range(3):
        known = meta[slab].reshape(gathered, 128)
        names = pltpu.roll(known, gathered - slots, 0)
        chosen = ((meta_row & 7) < slots) & (names == (meta_lane + 1).astype(F32))
        selector = chosen.astype(F32).T[:patch_rows].astype(BF16)
        selectors.append(selector)
        coarse_wave = placed_of(selector, known)
        diag = 6.0 / 16.0 - coarse_wave
        side = shift_imag * coarse_wave
        factor = omega_coarse / (diag * diag + side * side)
        coarse.append((coarse_wave, diag * factor, side * factor * sign))

    lane512 = iota((512, 128), 1)
    restrict = block_match(iota((512, 128), 0), lane512)
    grow = block_match(iota((128, 512), 1), iota((128, 512), 0))
    fine_lane = iota((fine_rows, 128), 1)
    same_x = ((iota((fine_rows, 128), 0) & 15) >> 2) == ((fine_lane >> 4) & 3)

    resid_real, resid_imag = add_ghosts(2, *resid)
    sums = times_selector(jnp.concatenate([resid_real, resid_imag], 1), restrict)
    sums = jnp.where(same_x, sums, 0.0) * (1.0 / 64.0)
    lines = [
        jnp.sum(sums[slot * 16 : slot * 16 + 16], axis=0, keepdims=True) for slot in range(slots)
    ]
    lines.append(jnp.zeros((8 - slots, 128), F32))
    rows[1, s] = jnp.concatenate(lines, 0)
    send_across(*coarse_exchange)
    send_slab(*coarse_exchange)

    lane_x = (lane >> 4) & 3
    lane_y = (lane >> 2) & 3
    lane_z = lane & 3
    patch_y = patch >> 2
    patch_z = patch & 3
    y_first = patch_y == 0
    y_last = patch_y >= rows_y - 1
    z_first = patch_z == 0
    z_last = patch_z == PZ - 1

    def turned(values, shift):
        return pltpu.roll(values, shift % 128, 1)

    def moved(values, shift):
        return pltpu.roll(values, shift % patch_rows, 0)

    def across(values, shift, outside):
        return jnp.where(outside, 0.0, moved(values, shift))

    def coarse_sum(lower, values, upper):
        x_down = turned(values, 16)
        x_up = turned(values, -16)
        edge = jnp.zeros_like(values) if lower is None else turned(lower, -48)
        total = jnp.where(lane_x == 0, edge, x_down)
        edge = jnp.zeros_like(values) if upper is None else turned(upper, 48)
        total = total + jnp.where(lane_x == 3, edge, x_up)
        total = total + jnp.where(
            lane_y == 0, turned(across(values, PZ, y_first), -12), turned(values, 4)
        )
        total = total + jnp.where(
            lane_y == 3, turned(across(values, -PZ, y_last), 12), turned(values, -4)
        )
        total = total + jnp.where(
            lane_z == 0, turned(across(values, 1, z_first), -3), turned(values, 1)
        )
        return total + jnp.where(
            lane_z == 3, turned(across(values, -1, z_last), 3), turned(values, -1)
        )

    def coarse_step(slab, values):
        _, near, cross = coarse[slab]
        return values * near + turned(values, 64) * cross

    receive_slab(*coarse_exchange)
    receive_across(*coarse_exchange)
    right = [
        placed_of(selectors[slab], rows[slab].reshape(gathered, 128)) for slab in range(3)
    ]
    there = [has_low.astype(F32), None, has_high.astype(F32)]

    def kept(slab, values):
        return values if there[slab] is None else values * there[slab]

    errors = [kept(slab, coarse_step(slab, right[slab])) for slab in range(3)]
    for sweep in range(CITER - 1):
        following = list(errors)
        for slab in (0, 1, 2) if sweep < CITER - 2 else (1,):
            values = errors[slab]
            lower = errors[slab - 1] if slab > 0 else None
            upper = errors[slab + 1] if slab < 2 else None
            coarse_wave = coarse[slab][0]
            applied = (6.0 * values - coarse_sum(lower, values, upper)) * (1.0 / 16.0)
            applied = applied - coarse_wave * (
                values + shift_imag * sign * turned(values, 64)
            )
            following[slab] = kept(
                slab, values + coarse_step(slab, right[slab] - applied)
            )
        errors = following

    placed_e[...] = errors[1]
    grown = []
    for slot in range(slots):
        line = placed_e[pl.ds(jnp.maximum(patch_of[slot], 0), 1), :]
        grown.append(jnp.broadcast_to(line, (16, 128)))
    grown = jnp.where(same_x, jnp.concatenate(grown, 0), 0.0)
    grown = times_selector(grown, grow)
    for slot in range(slots):
        live = patch_of[slot] >= 0
        span = slice(slot * 16, slot * 16 + 16)
        out_ref[slot, 0] = jnp.where(live, real[span] + grown[span, :256], 0.0)
        out_ref[slot, 1] = jnp.where(live, imag[span] + grown[span, 256:], 0.0)

    for stage in range(ROUNDS):
        sent_faces(stage)
        sent_across(*face_exchange(stage))
    for exchange in (meta_exchange, coarse_exchange):
        sent_slab(*exchange)
        sent_across(*exchange)


def body(n_grp, n_sub, field, source, patch_of_slot, neighbour, wave_index, wave_table):
    slots = field.shape[0]
    patch_rows = -(-3 * n_sub // 8) * 8
    stages = ROUNDS + 2
    smem = pl.BlockSpec(memory_space=pltpu.SMEM)
    vmem = pl.BlockSpec(memory_space=pltpu.VMEM)
    dma = pltpu.SemaphoreType.DMA((stages, n_sub))
    return pl.pallas_call(
        functools.partial(kernel, n_grp, n_sub),
        out_shape=jax.ShapeDtypeStruct(field.shape, F32),
        in_specs=[smem] * 4 + [pl.BlockSpec(memory_space=pltpu.HBM)] * 2,
        out_specs=vmem,
        scratch_shapes=[pltpu.VMEM(field.shape, F32)] * 2
        + [pltpu.SemaphoreType.DMA((2,))]
        + [pltpu.VMEM((n_sub * slots, 16, 128), F32)] * ROUNDS
        + [pltpu.VMEM((n_sub, 4 * slots, 128), F32)] * (2 * ROUNDS)
        + [
            pltpu.VMEM((ROUNDS, 2, 4 * slots, 128), F32),
            pltpu.VMEM((3, n_sub, 8, 128), F32),
            pltpu.VMEM((3, n_sub, 8, 128), F32),
            pltpu.VMEM((patch_rows, 128), F32),
        ]
        + [dma] * 6,
        compiler_params=pltpu.CompilerParams(
            collective_id=0, has_side_effects=True, vmem_limit_bytes=24 * 1024 * 1024
        ),
    )(
        *(
            pltpu.with_memory_space_constraint(values, pltpu.HBM)
            for values in (patch_of_slot, neighbour, wave_index, wave_table, field, source)
        ),
    )


def solution(mesh):
    return jax.shard_map(
        functools.partial(body, mesh.shape["grp"], mesh.shape["sub"]),
        mesh=mesh,
        in_specs=(
            P(("grp", "sub"), None, None, None),
            P(("grp", "sub"), None, None, None),
            P(("grp", "sub")),
            P(("grp", "sub"), None),
            P(("grp", "sub")),
            P(),
        ),
        out_specs=P(("grp", "sub"), None, None, None),
        check_vma=False,
    )
```

```python
import functools

import jax
import jax.numpy as jnp
from jax import lax
from jax.experimental import pallas as pl
from jax.experimental.pallas import tpu as pltpu
from jax.sharding import PartitionSpec as P

PZ = 4
CITER = 3
ROUNDS = 3

omega_fine = 0.7
omega_coarse = 0.6
shift_imag = 0.5

F32 = jnp.float32
BF16 = jnp.bfloat16
MESH = pl.DeviceIdType.MESH


def iota(shape, axis):
    return lax.broadcasted_iota(jnp.int32, shape, axis)


def terms_of(values, count):
    terms = []
    for _ in range(count - 1):
        term = values.astype(BF16)
        terms.append(term)
        values = values - term.astype(F32)
    terms.append(values.astype(BF16))
    return terms


def times_selector(values, selector, count=2):
    rows = values.shape[0]
    stacked = jnp.concatenate(terms_of(values, count), 0)
    product = jnp.dot(stacked, selector, preferred_element_type=F32)
    total = product[:rows]
    for term in range(1, count):
        total = total + product[term * rows : (term + 1) * rows]
    return total


def face_cells(shape, lane_axis, opposite):
    lane = iota(shape, lane_axis)
    face = lane >> 5
    if opposite:
        face = face ^ 1
    place = lane & 15
    cell = jnp.where(
        face < 2,
        place + jnp.where(face == 1, 240, 0),
        place * 16 + jnp.where(face == 3, 15, 0),
    )
    return (lane >> 4) & 1, cell


def pack_matrix():
    shape = (512, 128)
    part, cell = face_cells(shape, 1, False)
    return (iota(shape, 0) == part * 256 + cell).astype(F32).astype(BF16)


def unpack_matrix():
    shape = (128, 512)
    part, cell = face_cells(shape, 0, True)
    return (iota(shape, 1) == part * 256 + cell).astype(F32).astype(BF16)


def block_match(fine, lane):
    same_part = (fine >> 8) == (lane >> 6)
    same_y = ((fine >> 6) & 3) == ((lane >> 2) & 3)
    same_z = ((fine >> 2) & 3) == (lane & 3)
    return (same_part & same_y & same_z).astype(F32).astype(BF16)


def kernel(
    n_grp,
    n_sub,
    patch_ref,
    link_ref,
    index_ref,
    table_ref,
    field_in,
    source_in,
    out_ref,
    field_ref,
    source_ref,
    input_sem,
    faces_0,
    faces_1,
    faces_2,
    below_0,
    below_1,
    below_2,
    above_0,
    above_1,
    above_2,
    sheets,
    meta,
    rows,
    placed_e,
    slab_send,
    slab_recv,
    low_send,
    low_recv,
    high_send,
    high_recv,
):
    faces = (faces_0, faces_1, faces_2)
    below = (below_0, below_1, below_2)
    above = (above_0, above_1, above_2)
    slots = field_ref.shape[0]
    fine_rows = slots * 16
    patch_total = 3 * n_sub
    rows_y = patch_total // PZ
    patch_rows = -(-patch_total // 8) * 8
    g = lax.axis_index("grp")
    s = lax.axis_index("sub")
    has_low = g > 0
    has_high = g < n_grp - 1

    def beside(step):
        return lax.rem(s + step, n_sub)

    def before(step):
        return lax.rem(s + n_sub - step, n_sub)

    field_copy = pltpu.make_async_copy(field_in, field_ref, input_sem.at[0])
    source_copy = pltpu.make_async_copy(source_in, source_ref, input_sem.at[1])
    field_copy.start()
    source_copy.start()

    barrier = pltpu.get_barrier_semaphore()
    for step in range(1, n_sub):
        pl.semaphore_signal(barrier, inc=1, device_id=(g, beside(step)), device_id_type=MESH)

    @pl.when(has_low)
    def _():
        for step in range(n_sub):
            pl.semaphore_signal(
                barrier, inc=1, device_id=(g - 1, beside(step)), device_id_type=MESH
            )

    @pl.when(has_high)
    def _():
        for step in range(n_sub):
            pl.semaphore_signal(
                barrier, inc=1, device_id=(g + 1, beside(step)), device_id_type=MESH
            )

    def slab_copy(ref_of, stage, step, owner):
        ref = ref_of(owner)
        return pltpu.make_async_remote_copy(
            src_ref=ref,
            dst_ref=ref,
            send_sem=slab_send.at[stage, step],
            recv_sem=slab_recv.at[stage, step],
            device_id=(g, beside(step)),
            device_id_type=MESH,
        )

    def low_copy(src, dst, stage, step):
        return pltpu.make_async_remote_copy(
            src_ref=src,
            dst_ref=dst,
            send_sem=low_send.at[stage, step],
            recv_sem=high_recv.at[stage, step],
            device_id=(g - 1, beside(step)),
            device_id_type=MESH,
        )

    def high_copy(src, dst, stage, step):
        return pltpu.make_async_remote_copy(
            src_ref=src,
            dst_ref=dst,
            send_sem=high_send.at[stage, step],
            recv_sem=low_recv.at[stage, step],
            device_id=(g + 1, beside(step)),
            device_id_type=MESH,
        )

    other = s + 1 - 2 * lax.rem(s, 2)

    def face_copy(stage, owner, to, sem):
        ref = faces[stage].at[pl.ds(owner * slots, slots)]
        return pltpu.make_async_remote_copy(
            src_ref=ref,
            dst_ref=ref,
            send_sem=slab_send.at[stage, sem],
            recv_sem=slab_recv.at[stage, sem],
            device_id=(g, to),
            device_id_type=MESH,
        )

    def send_faces(stage):
        for step in range(2, n_sub, 2):
            face_copy(stage, s, beside(step), step).start()
        face_copy(stage, s, other, 1).start()

    def forward_faces(stage):
        for step in range(2, n_sub, 2):
            face_copy(stage, before(step), other, step).wait_recv()
            face_copy(stage, before(step), other, step + 1).start()

    def receive_faces(stage):
        face_copy(stage, other, other, 1).wait_recv()
        for step in range(2, n_sub, 2):
            owner = lax.rem(other + n_sub - step, n_sub)
            face_copy(stage, owner, other, step + 1).wait_recv()

    def sent_faces(stage):
        for step in range(2, n_sub, 2):
            face_copy(stage, s, beside(step), step).wait_send()
            face_copy(stage, before(step), other, step + 1).wait_send()
        face_copy(stage, s, other, 1).wait_send()

    def sent_all(stage):
        sent_faces(stage)
        sent_across(*face_exchange(stage))

    def send_slab(stage, slab_of, *_):
        for step in range(1, n_sub):
            slab_copy(slab_of, stage, step, s).start()

    def send_across(stage, slab_of, low_src, low_of, high_src, high_of):
        @pl.when(has_high)
        def _():
            for step in range(n_sub):
                high_copy(high_src, low_of(s), stage, step).start()

        @pl.when(has_low)
        def _():
            for step in range(n_sub):
                low_copy(low_src, high_of(s), stage, step).start()

    def receive_slab(stage, slab_of, *_):
        for step in range(1, n_sub):
            slab_copy(slab_of, stage, step, before(step)).wait_recv()

    def receive_across(stage, slab_of, low_src, low_of, high_src, high_of):
        @pl.when(has_low)
        def _():
            for step in range(n_sub):
                high_copy(high_src, low_of(before(step)), stage, step).wait_recv()

        @pl.when(has_high)
        def _():
            for step in range(n_sub):
                low_copy(low_src, high_of(before(step)), stage, step).wait_recv()

    def sent_slab(stage, slab_of, *_):
        for step in range(1, n_sub):
            slab_copy(slab_of, stage, step, s).wait_send()

    def sent_across(stage, slab_of, low_src, low_of, high_src, high_of):
        @pl.when(has_high)
        def _():
            for step in range(n_sub):
                high_copy(high_src, low_of(s), stage, step).wait_send()

        @pl.when(has_low)
        def _():
            for step in range(n_sub):
                low_copy(low_src, high_of(s), stage, step).wait_send()

    def face_exchange(stage):
        return (
            stage,
            None,
            sheets.at[stage, 0],
            lambda owner: below[stage].at[owner],
            sheets.at[stage, 1],
            lambda owner: above[stage].at[owner],
        )

    def row_exchange(stage, ref):
        mine = ref.at[1, s]
        return (
            stage,
            lambda owner: ref.at[1, owner],
            mine,
            lambda owner: ref.at[0, owner],
            mine,
            lambda owner: ref.at[2, owner],
        )

    meta_exchange = row_exchange(ROUNDS, meta)
    coarse_exchange = row_exchange(ROUNDS + 1, rows)

    @pl.when(jnp.logical_not(has_low))
    def _():
        for layers in below:
            layers[...] = jnp.zeros_like(layers)
        meta[0] = jnp.zeros_like(meta[0])
        rows[0] = jnp.zeros_like(rows[0])

    @pl.when(jnp.logical_not(has_high))
    def _():
        for layers in above:
            layers[...] = jnp.zeros_like(layers)
        meta[2] = jnp.zeros_like(meta[2])
        rows[2] = jnp.zeros_like(rows[2])

    wave_of = [table_ref[index_ref[slot]] for slot in range(slots)]
    patch_of = [patch_ref[slot] for slot in range(slots)]

    row8 = iota((8, 128), 0)
    meta_rows = jnp.zeros((8, 128), F32)
    for slot in range(slots):
        meta_rows = jnp.where(row8 == slot, wave_of[slot], meta_rows)
        meta_rows = jnp.where(
            row8 == slots + slot, (patch_of[slot] + 1).astype(F32), meta_rows
        )
    meta[1, s] = meta_rows

    def joined(ref, part):
        return jnp.concatenate([ref[slot, part] for slot in range(slots)], 0)

    pack = pack_matrix()
    field_copy.wait()
    real = joined(field_ref, 0)
    imag = joined(field_ref, 1)

    def put_sheets(stage, real, imag):
        for side, edge_row in ((0, 0), (1, 15)):
            lines = []
            for half in range(2):
                for slot in range(slots):
                    for values in (real, imag):
                        row = slot * 16 + edge_row
                        lines.append(values[row : row + 1, half * 128 : half * 128 + 128])
            sheets[stage, side] = jnp.concatenate(lines, 0)

    def put_faces(stage, real, imag):
        packed = times_selector(jnp.concatenate([real, imag], 1), pack)
        for slot in range(slots):
            faces[stage][s * slots + slot] = packed[slot * 16 : slot * 16 + 16]

    put_sheets(0, real, imag)
    put_faces(0, real, imag)

    greeted = n_sub - 1 + n_sub * (has_low.astype(jnp.int32) + has_high.astype(jnp.int32))
    pl.semaphore_wait(barrier, greeted)

    send_faces(0)
    send_across(*face_exchange(0))
    send_slab(*meta_exchange)
    send_across(*meta_exchange)

    source_copy.wait()
    source_real = joined(source_ref, 0)
    source_imag = joined(source_ref, 1)
    unpack = unpack_matrix()
    wave = jnp.concatenate([jnp.full((16, 256), wave_of[slot], F32) for slot in range(slots)], 0)
    real_diag = 6.0 - wave
    imag_diag = shift_imag * wave
    scale = omega_fine / (real_diag * real_diag + imag_diag * imag_diag)
    step_real = real_diag * scale
    step_imag = imag_diag * scale

    cell = iota((fine_rows, 256), 1)
    fine_i = iota((fine_rows, 256), 0) & 15
    y_low = cell < 16
    y_high = cell >= 240
    z_low = (cell & 15) == 0
    z_high = (cell & 15) == 15
    x_low = fine_i == 0
    x_high = fine_i == 15

    def inner_sum(values):
        total = jnp.where(y_low, 0.0, pltpu.roll(values, 16, 1))
        total = total + jnp.where(y_high, 0.0, pltpu.roll(values, 240, 1))
        total = total + jnp.where(z_low, 0.0, pltpu.roll(values, 1, 1))
        total = total + jnp.where(z_high, 0.0, pltpu.roll(values, 255, 1))
        total = total + jnp.where(x_low, 0.0, pltpu.roll(values, 1, 0))
        return total + jnp.where(x_high, 0.0, pltpu.roll(values, fine_rows - 1, 0))

    def local_part(real, imag):
        out_real = (
            source_real
            + inner_sum(real)
            - (6.0 * real - wave * (real - shift_imag * imag))
        )
        out_imag = (
            source_imag
            + inner_sum(imag)
            - (6.0 * imag - wave * (imag + shift_imag * real))
        )
        return out_real, out_imag

    links = [[link_ref[slot, face] for face in range(6)] for slot in range(slots)]
    safe = [[jnp.maximum(link, 0) for link in line] for line in links]
    valid = [[(link >= 0).astype(F32) for link in line] for line in links]
    packed_lane = iota((16, 128), 1) >> 5
    row16 = iota((16, 256), 0)

    def add_ghosts(stage, out_real, out_imag):
        receive_faces(stage)
        blocks = []
        for slot in range(slots):
            got = [
                faces[stage][safe[slot][face]] * valid[slot][face] for face in range(2, 6)
            ]
            blocks.append(
                jnp.where(
                    packed_lane == 1,
                    got[0],
                    jnp.where(
                        packed_lane == 0,
                        got[1],
                        jnp.where(packed_lane == 3, got[2], got[3]),
                    ),
                )
            )
        spread = times_selector(jnp.concatenate(blocks, 0), unpack)
        out_real = out_real + spread[:, :256]
        out_imag = out_imag + spread[:, 256:]
        receive_across(*face_exchange(stage))
        result = []
        for part, own in ((0, out_real), (1, out_imag)):
            layers = []
            for slot in range(slots):
                layer = jnp.zeros((16, 256), F32)
                for face, ref, at in ((0, below, 0), (1, above, 15)):
                    link = safe[slot][face]
                    owner = link >> 2
                    first = (link & 3) * 2 + part
                    line = jnp.concatenate(
                        [
                            ref[stage][owner, pl.ds(first, 1), :],
                            ref[stage][owner, pl.ds(first + 8, 1), :],
                        ],
                        1,
                    )
                    layer = jnp.where(row16 == at, line * valid[slot][face], layer)
                layers.append(layer)
            result.append(own + jnp.concatenate(layers, 0))
        return result

    for stage in range(2):
        resid = local_part(real, imag)
        forward_faces(stage)
        if stage:
            sent_all(stage - 1)
        resid_real, resid_imag = add_ghosts(stage, *resid)
        real, imag = (
            real + (resid_real * step_real - resid_imag * step_imag),
            imag + (resid_real * step_imag + resid_imag * step_real),
        )
        put_sheets(stage + 1, real, imag)
        send_across(*face_exchange(stage + 1))
        put_faces(stage + 1, real, imag)
        send_faces(stage + 1)

    resid = local_part(real, imag)
    forward_faces(2)
    sent_all(1)
    sent_slab(*meta_exchange)
    sent_across(*meta_exchange)
    receive_slab(*meta_exchange)
    receive_across(*meta_exchange)
    gathered = n_sub * 8
    meta_row = iota((gathered, 128), 0)
    meta_lane = iota((gathered, 128), 1)
    selectors = []
    coarse = []
    lane = iota((patch_rows, 128), 1)
    patch = iota((patch_rows, 128), 0)
    sign = jnp.where(lane < 64, -1.0, 1.0)

    def placed_of(selector, values):
        terms = jnp.concatenate(terms_of(values, 3), 1)
        product = jnp.dot(selector, terms, preferred_element_type=F32)
        return product[:, :128] + product[:, 128:256] + product[:, 256:]

    for slab in range(3):
        known = meta[slab].reshape(gathered, 128)
        names = pltpu.roll(known, gathered - slots, 0)
        chosen = ((meta_row & 7) < slots) & (names == (meta_lane + 1).astype(F32))
        selector = chosen.astype(F32).T[:patch_rows].astype(BF16)
        selectors.append(selector)
        coarse_wave = placed_of(selector, known)
        diag = 6.0 / 16.0 - coarse_wave
        side = shift_imag * coarse_wave
        factor = omega_coarse / (diag * diag + side * side)
        coarse.append((coarse_wave, diag * factor, side * factor * sign))

    lane512 = iota((512, 128), 1)
    restrict = block_match(iota((512, 128), 0), lane512)
    grow = block_match(iota((128, 512), 1), iota((128, 512), 0))
    fine_lane = iota((fine_rows, 128), 1)
    same_x = ((iota((fine_rows, 128), 0) & 15) >> 2) == ((fine_lane >> 4) & 3)

    resid_real, resid_imag = add_ghosts(2, *resid)
    sums = times_selector(jnp.concatenate([resid_real, resid_imag], 1), restrict)
    sums = jnp.where(same_x, sums, 0.0) * (1.0 / 64.0)
    lines = [
        jnp.sum(sums[slot * 16 : slot * 16 + 16], axis=0, keepdims=True) for slot in range(slots)
    ]
    lines.append(jnp.zeros((8 - slots, 128), F32))
    rows[1, s] = jnp.concatenate(lines, 0)
    send_across(*coarse_exchange)
    send_slab(*coarse_exchange)

    sent_all(2)
    sent_slab(*coarse_exchange)
    sent_across(*coarse_exchange)

    lane_x = (lane >> 4) & 3
    lane_y = (lane >> 2) & 3
    lane_z = lane & 3
    patch_y = patch >> 2
    patch_z = patch & 3
    y_first = patch_y == 0
    y_last = patch_y >= rows_y - 1
    z_first = patch_z == 0
    z_last = patch_z == PZ - 1

    def turned(values, shift):
        return pltpu.roll(values, shift % 128, 1)

    def moved(values, shift):
        return pltpu.roll(values, shift % patch_rows, 0)

    def across(values, shift, outside):
        return jnp.where(outside, 0.0, moved(values, shift))

    def coarse_sum(lower, values, upper):
        x_down = turned(values, 16)
        x_up = turned(values, -16)
        edge = jnp.zeros_like(values) if lower is None else turned(lower, -48)
        total = jnp.where(lane_x == 0, edge, x_down)
        edge = jnp.zeros_like(values) if upper is None else turned(upper, 48)
        total = total + jnp.where(lane_x == 3, edge, x_up)
        total = total + jnp.where(
            lane_y == 0, turned(across(values, PZ, y_first), -12), turned(values, 4)
        )
        total = total + jnp.where(
            lane_y == 3, turned(across(values, -PZ, y_last), 12), turned(values, -4)
        )
        total = total + jnp.where(
            lane_z == 0, turned(across(values, 1, z_first), -3), turned(values, 1)
        )
        return total + jnp.where(
            lane_z == 3, turned(across(values, -1, z_last), 3), turned(values, -1)
        )

    def coarse_step(slab, values):
        _, near, cross = coarse[slab]
        return values * near + turned(values, 64) * cross

    receive_slab(*coarse_exchange)
    receive_across(*coarse_exchange)
    right = [
        placed_of(selectors[slab], rows[slab].reshape(gathered, 128)) for slab in range(3)
    ]
    there = [has_low.astype(F32), None, has_high.astype(F32)]

    def kept(slab, values):
        return values if there[slab] is None else values * there[slab]

    errors = [kept(slab, coarse_step(slab, right[slab])) for slab in range(3)]
    for sweep in range(CITER - 1):
        following = list(errors)
        for slab in (0, 1, 2) if sweep < CITER - 2 else (1,):
            values = errors[slab]
            lower = errors[slab - 1] if slab > 0 else None
            upper = errors[slab + 1] if slab < 2 else None
            coarse_wave = coarse[slab][0]
            applied = (6.0 * values - coarse_sum(lower, values, upper)) * (1.0 / 16.0)
            applied = applied - coarse_wave * (
                values + shift_imag * sign * turned(values, 64)
            )
            following[slab] = kept(
                slab, values + coarse_step(slab, right[slab] - applied)
            )
        errors = following

    placed_e[...] = errors[1]
    grown = []
    for slot in range(slots):
        line = placed_e[pl.ds(jnp.maximum(patch_of[slot], 0), 1), :]
        grown.append(jnp.broadcast_to(line, (16, 128)))
    grown = jnp.where(same_x, jnp.concatenate(grown, 0), 0.0)
    grown = times_selector(grown, grow)
    for slot in range(slots):
        live = patch_of[slot] >= 0
        span = slice(slot * 16, slot * 16 + 16)
        out_ref[slot, 0] = jnp.where(live, real[span] + grown[span, :256], 0.0)
        out_ref[slot, 1] = jnp.where(live, imag[span] + grown[span, 256:], 0.0)


def body(n_grp, n_sub, field, source, patch_of_slot, neighbour, wave_index, wave_table):
    slots = field.shape[0]
    patch_rows = -(-3 * n_sub // 8) * 8
    stages = ROUNDS + 2
    smem = pl.BlockSpec(memory_space=pltpu.SMEM)
    vmem = pl.BlockSpec(memory_space=pltpu.VMEM)
    dma = pltpu.SemaphoreType.DMA((stages, n_sub))
    return pl.pallas_call(
        functools.partial(kernel, n_grp, n_sub),
        out_shape=jax.ShapeDtypeStruct(field.shape, F32),
        in_specs=[smem] * 4 + [pl.BlockSpec(memory_space=pltpu.HBM)] * 2,
        out_specs=vmem,
        scratch_shapes=[pltpu.VMEM(field.shape, F32)] * 2
        + [pltpu.SemaphoreType.DMA((2,))]
        + [pltpu.VMEM((n_sub * slots, 16, 128), F32)] * ROUNDS
        + [pltpu.VMEM((n_sub, 4 * slots, 128), F32)] * (2 * ROUNDS)
        + [
            pltpu.VMEM((ROUNDS, 2, 4 * slots, 128), F32),
            pltpu.VMEM((3, n_sub, 8, 128), F32),
            pltpu.VMEM((3, n_sub, 8, 128), F32),
            pltpu.VMEM((patch_rows, 128), F32),
        ]
        + [dma] * 6,
        compiler_params=pltpu.CompilerParams(
            collective_id=0, has_side_effects=True, vmem_limit_bytes=24 * 1024 * 1024
        ),
    )(
        *(
            pltpu.with_memory_space_constraint(values, pltpu.HBM)
            for values in (patch_of_slot, neighbour, wave_index, wave_table, field, source)
        ),
    )


def solution(mesh):
    return jax.shard_map(
        functools.partial(body, mesh.shape["grp"], mesh.shape["sub"]),
        mesh=mesh,
        in_specs=(
            P(("grp", "sub"), None, None, None),
            P(("grp", "sub"), None, None, None),
            P(("grp", "sub")),
            P(("grp", "sub"), None),
            P(("grp", "sub")),
            P(),
        ),
        out_specs=P(("grp", "sub"), None, None, None),
        check_vma=False,
    )
```

```python
import functools

import jax
import jax.numpy as jnp
from jax import lax
from jax.experimental import pallas as pl
from jax.experimental.pallas import tpu as pltpu
from jax.sharding import PartitionSpec as P

PZ = 4
CITER = 3
ROUNDS = 3

omega_fine = 0.7
omega_coarse = 0.6
shift_imag = 0.5

F32 = jnp.float32
BF16 = jnp.bfloat16
MESH = pl.DeviceIdType.MESH


def iota(shape, axis):
    return lax.broadcasted_iota(jnp.int32, shape, axis)


def terms_of(values, count):
    terms = []
    for _ in range(count - 1):
        term = values.astype(BF16)
        terms.append(term)
        values = values - term.astype(F32)
    terms.append(values.astype(BF16))
    return terms


def times_selector(values, selector, count=2):
    rows = values.shape[0]
    stacked = jnp.concatenate(terms_of(values, count), 0)
    product = jnp.dot(stacked, selector, preferred_element_type=F32)
    total = product[:rows]
    for term in range(1, count):
        total = total + product[term * rows : (term + 1) * rows]
    return total


def face_cells(shape, lane_axis, opposite):
    lane = iota(shape, lane_axis)
    face = lane >> 5
    if opposite:
        face = face ^ 1
    place = lane & 15
    cell = jnp.where(
        face < 2,
        place + jnp.where(face == 1, 240, 0),
        place * 16 + jnp.where(face == 3, 15, 0),
    )
    return (lane >> 4) & 1, cell


def pack_matrix():
    shape = (512, 128)
    part, cell = face_cells(shape, 1, False)
    return (iota(shape, 0) == part * 256 + cell).astype(F32).astype(BF16)


def unpack_matrix():
    shape = (128, 512)
    part, cell = face_cells(shape, 0, True)
    return (iota(shape, 1) == part * 256 + cell).astype(F32).astype(BF16)


def block_match(fine, lane):
    same_part = (fine >> 8) == (lane >> 6)
    same_y = ((fine >> 6) & 3) == ((lane >> 2) & 3)
    same_z = ((fine >> 2) & 3) == (lane & 3)
    return (same_part & same_y & same_z).astype(F32).astype(BF16)


def kernel(
    n_grp,
    n_sub,
    patch_ref,
    link_ref,
    index_ref,
    table_ref,
    field_in,
    source_in,
    out_ref,
    field_ref,
    source_ref,
    input_sem,
    faces_0,
    faces_1,
    faces_2,
    below_0,
    below_1,
    below_2,
    above_0,
    above_1,
    above_2,
    sheets,
    meta,
    rows,
    placed_e,
    slab_send,
    slab_recv,
    low_send,
    low_recv,
    high_send,
    high_recv,
):
    faces = (faces_0, faces_1, faces_2)
    below = (below_0, below_1, below_2)
    above = (above_0, above_1, above_2)
    slots = field_ref.shape[0]
    fine_rows = slots * 16
    patch_total = 3 * n_sub
    rows_y = patch_total // PZ
    patch_rows = -(-patch_total // 8) * 8
    g = lax.axis_index("grp")
    s = lax.axis_index("sub")
    has_low = g > 0
    has_high = g < n_grp - 1

    def beside(step):
        return lax.rem(s + step, n_sub)

    def before(step):
        return lax.rem(s + n_sub - step, n_sub)

    field_copy = pltpu.make_async_copy(field_in, field_ref, input_sem.at[0])
    source_copy = pltpu.make_async_copy(source_in, source_ref, input_sem.at[1])
    field_copy.start()
    source_copy.start()

    barrier = pltpu.get_barrier_semaphore()
    for step in range(1, n_sub):
        pl.semaphore_signal(barrier, inc=1, device_id=(g, beside(step)), device_id_type=MESH)

    @pl.when(has_low)
    def _():
        for step in range(n_sub):
            pl.semaphore_signal(
                barrier, inc=1, device_id=(g - 1, beside(step)), device_id_type=MESH
            )

    @pl.when(has_high)
    def _():
        for step in range(n_sub):
            pl.semaphore_signal(
                barrier, inc=1, device_id=(g + 1, beside(step)), device_id_type=MESH
            )

    def slab_copy(ref_of, stage, step, owner):
        ref = ref_of(owner)
        return pltpu.make_async_remote_copy(
            src_ref=ref,
            dst_ref=ref,
            send_sem=slab_send.at[stage, step],
            recv_sem=slab_recv.at[stage, step],
            device_id=(g, beside(step)),
            device_id_type=MESH,
        )

    def low_copy(src, dst, stage, step):
        return pltpu.make_async_remote_copy(
            src_ref=src,
            dst_ref=dst,
            send_sem=low_send.at[stage, step],
            recv_sem=high_recv.at[stage, step],
            device_id=(g - 1, beside(step)),
            device_id_type=MESH,
        )

    def high_copy(src, dst, stage, step):
        return pltpu.make_async_remote_copy(
            src_ref=src,
            dst_ref=dst,
            send_sem=high_send.at[stage, step],
            recv_sem=low_recv.at[stage, step],
            device_id=(g + 1, beside(step)),
            device_id_type=MESH,
        )

    other = s + 1 - 2 * lax.rem(s, 2)

    def face_copy(stage, owner, to, sem):
        ref = faces[stage].at[pl.ds(owner * slots, slots)]
        return pltpu.make_async_remote_copy(
            src_ref=ref,
            dst_ref=ref,
            send_sem=slab_send.at[stage, sem],
            recv_sem=slab_recv.at[stage, sem],
            device_id=(g, to),
            device_id_type=MESH,
        )

    def send_faces(stage):
        for step in range(2, n_sub, 2):
            face_copy(stage, s, beside(step), step).start()
        face_copy(stage, s, other, 1).start()

    def forward_faces(stage):
        for step in range(2, n_sub, 2):
            face_copy(stage, before(step), other, step).wait_recv()
            face_copy(stage, before(step), other, step + 1).start()

    def receive_faces(stage):
        face_copy(stage, other, other, 1).wait_recv()
        for step in range(2, n_sub, 2):
            owner = lax.rem(other + n_sub - step, n_sub)
            face_copy(stage, owner, other, step + 1).wait_recv()

    def sent_faces(stage):
        for step in range(2, n_sub, 2):
            face_copy(stage, s, beside(step), step).wait_send()
            face_copy(stage, before(step), other, step + 1).wait_send()
        face_copy(stage, s, other, 1).wait_send()

    def layer_copy(ref, owner, sends, recvs, stage, sem):
        return pltpu.make_async_remote_copy(
            src_ref=ref[stage].at[owner],
            dst_ref=ref[stage].at[owner],
            send_sem=sends.at[stage, sem],
            recv_sem=recvs.at[stage, sem],
            device_id=(g, other),
            device_id_type=MESH,
        )

    def low_layers(owner, stage, sem):
        return layer_copy(below, owner, low_send, low_recv, stage, sem)

    def high_layers(owner, stage, sem):
        return layer_copy(above, owner, high_send, high_recv, stage, sem)

    def send_layers(stage):
        @pl.when(has_high)
        def _():
            for step in range(0, n_sub, 2):
                high_copy(sheets.at[stage, 1], below[stage].at[s], stage, step).start()

        @pl.when(has_low)
        def _():
            for step in range(0, n_sub, 2):
                low_copy(sheets.at[stage, 0], above[stage].at[s], stage, step).start()

    def forward_layers(stage):
        @pl.when(has_low)
        def _():
            for step in range(0, n_sub, 2):
                low_layers(before(step), stage, step).wait_recv()
                low_layers(before(step), stage, step + 1).start()

        @pl.when(has_high)
        def _():
            for step in range(0, n_sub, 2):
                high_layers(before(step), stage, step).wait_recv()
                high_layers(before(step), stage, step + 1).start()

    def receive_layers(stage):
        @pl.when(has_low)
        def _():
            for step in range(0, n_sub, 2):
                owner = lax.rem(other + n_sub - step, n_sub)
                low_layers(owner, stage, step + 1).wait_recv()

        @pl.when(has_high)
        def _():
            for step in range(0, n_sub, 2):
                owner = lax.rem(other + n_sub - step, n_sub)
                high_layers(owner, stage, step + 1).wait_recv()

    def sent_layers(stage):
        @pl.when(has_high)
        def _():
            for step in range(0, n_sub, 2):
                high_copy(sheets.at[stage, 1], below[stage].at[s], stage, step).wait_send()
                high_layers(before(step), stage, step + 1).wait_send()

        @pl.when(has_low)
        def _():
            for step in range(0, n_sub, 2):
                low_copy(sheets.at[stage, 0], above[stage].at[s], stage, step).wait_send()
                low_layers(before(step), stage, step + 1).wait_send()

    def sent_all(stage):
        sent_faces(stage)
        sent_layers(stage)

    def send_slab(stage, slab_of, *_):
        for step in range(1, n_sub):
            slab_copy(slab_of, stage, step, s).start()

    def send_across(stage, slab_of, low_src, low_of, high_src, high_of):
        @pl.when(has_high)
        def _():
            for step in range(n_sub):
                high_copy(high_src, low_of(s), stage, step).start()

        @pl.when(has_low)
        def _():
            for step in range(n_sub):
                low_copy(low_src, high_of(s), stage, step).start()

    def receive_slab(stage, slab_of, *_):
        for step in range(1, n_sub):
            slab_copy(slab_of, stage, step, before(step)).wait_recv()

    def receive_across(stage, slab_of, low_src, low_of, high_src, high_of):
        @pl.when(has_low)
        def _():
            for step in range(n_sub):
                high_copy(high_src, low_of(before(step)), stage, step).wait_recv()

        @pl.when(has_high)
        def _():
            for step in range(n_sub):
                low_copy(low_src, high_of(before(step)), stage, step).wait_recv()

    def sent_slab(stage, slab_of, *_):
        for step in range(1, n_sub):
            slab_copy(slab_of, stage, step, s).wait_send()

    def sent_across(stage, slab_of, low_src, low_of, high_src, high_of):
        @pl.when(has_high)
        def _():
            for step in range(n_sub):
                high_copy(high_src, low_of(s), stage, step).wait_send()

        @pl.when(has_low)
        def _():
            for step in range(n_sub):
                low_copy(low_src, high_of(s), stage, step).wait_send()

    def row_exchange(stage, ref):
        mine = ref.at[1, s]
        return (
            stage,
            lambda owner: ref.at[1, owner],
            mine,
            lambda owner: ref.at[0, owner],
            mine,
            lambda owner: ref.at[2, owner],
        )

    meta_exchange = row_exchange(ROUNDS, meta)
    coarse_exchange = row_exchange(ROUNDS + 1, rows)

    @pl.when(jnp.logical_not(has_low))
    def _():
        for layers in below:
            layers[...] = jnp.zeros_like(layers)
        meta[0] = jnp.zeros_like(meta[0])
        rows[0] = jnp.zeros_like(rows[0])

    @pl.when(jnp.logical_not(has_high))
    def _():
        for layers in above:
            layers[...] = jnp.zeros_like(layers)
        meta[2] = jnp.zeros_like(meta[2])
        rows[2] = jnp.zeros_like(rows[2])

    wave_of = [table_ref[index_ref[slot]] for slot in range(slots)]
    patch_of = [patch_ref[slot] for slot in range(slots)]

    row8 = iota((8, 128), 0)
    meta_rows = jnp.zeros((8, 128), F32)
    for slot in range(slots):
        meta_rows = jnp.where(row8 == slot, wave_of[slot], meta_rows)
        meta_rows = jnp.where(
            row8 == slots + slot, (patch_of[slot] + 1).astype(F32), meta_rows
        )
    meta[1, s] = meta_rows

    def joined(ref, part):
        return jnp.concatenate([ref[slot, part] for slot in range(slots)], 0)

    pack = pack_matrix()
    field_copy.wait()
    real = joined(field_ref, 0)
    imag = joined(field_ref, 1)

    def put_sheets(stage, real, imag):
        for side, edge_row in ((0, 0), (1, 15)):
            lines = []
            for half in range(2):
                for slot in range(slots):
                    for values in (real, imag):
                        row = slot * 16 + edge_row
                        lines.append(values[row : row + 1, half * 128 : half * 128 + 128])
            sheets[stage, side] = jnp.concatenate(lines, 0)

    def put_faces(stage, real, imag):
        packed = times_selector(jnp.concatenate([real, imag], 1), pack)
        for slot in range(slots):
            faces[stage][s * slots + slot] = packed[slot * 16 : slot * 16 + 16]

    put_sheets(0, real, imag)
    put_faces(0, real, imag)

    greeted = n_sub - 1 + n_sub * (has_low.astype(jnp.int32) + has_high.astype(jnp.int32))
    pl.semaphore_wait(barrier, greeted)

    send_faces(0)
    send_layers(0)
    send_slab(*meta_exchange)
    send_across(*meta_exchange)

    source_copy.wait()
    source_real = joined(source_ref, 0)
    source_imag = joined(source_ref, 1)
    unpack = unpack_matrix()
    wave = jnp.concatenate([jnp.full((16, 256), wave_of[slot], F32) for slot in range(slots)], 0)
    real_diag = 6.0 - wave
    imag_diag = shift_imag * wave
    scale = omega_fine / (real_diag * real_diag + imag_diag * imag_diag)
    step_real = real_diag * scale
    step_imag = imag_diag * scale

    cell = iota((fine_rows, 256), 1)
    fine_i = iota((fine_rows, 256), 0) & 15
    y_low = cell < 16
    y_high = cell >= 240
    z_low = (cell & 15) == 0
    z_high = (cell & 15) == 15
    x_low = fine_i == 0
    x_high = fine_i == 15

    def inner_sum(values):
        total = jnp.where(y_low, 0.0, pltpu.roll(values, 16, 1))
        total = total + jnp.where(y_high, 0.0, pltpu.roll(values, 240, 1))
        total = total + jnp.where(z_low, 0.0, pltpu.roll(values, 1, 1))
        total = total + jnp.where(z_high, 0.0, pltpu.roll(values, 255, 1))
        total = total + jnp.where(x_low, 0.0, pltpu.roll(values, 1, 0))
        return total + jnp.where(x_high, 0.0, pltpu.roll(values, fine_rows - 1, 0))

    def local_part(real, imag):
        out_real = (
            source_real
            + inner_sum(real)
            - (6.0 * real - wave * (real - shift_imag * imag))
        )
        out_imag = (
            source_imag
            + inner_sum(imag)
            - (6.0 * imag - wave * (imag + shift_imag * real))
        )
        return out_real, out_imag

    links = [[link_ref[slot, face] for face in range(6)] for slot in range(slots)]
    safe = [[jnp.maximum(link, 0) for link in line] for line in links]
    valid = [[(link >= 0).astype(F32) for link in line] for line in links]
    packed_lane = iota((16, 128), 1) >> 5
    row16 = iota((16, 256), 0)

    def add_ghosts(stage, out_real, out_imag):
        receive_faces(stage)
        blocks = []
        for slot in range(slots):
            got = [
                faces[stage][safe[slot][face]] * valid[slot][face] for face in range(2, 6)
            ]
            blocks.append(
                jnp.where(
                    packed_lane == 1,
                    got[0],
                    jnp.where(
                        packed_lane == 0,
                        got[1],
                        jnp.where(packed_lane == 3, got[2], got[3]),
                    ),
                )
            )
        spread = times_selector(jnp.concatenate(blocks, 0), unpack)
        out_real = out_real + spread[:, :256]
        out_imag = out_imag + spread[:, 256:]
        receive_layers(stage)
        result = []
        for part, own in ((0, out_real), (1, out_imag)):
            layers = []
            for slot in range(slots):
                layer = jnp.zeros((16, 256), F32)
                for face, ref, at in ((0, below, 0), (1, above, 15)):
                    link = safe[slot][face]
                    owner = link >> 2
                    first = (link & 3) * 2 + part
                    line = jnp.concatenate(
                        [
                            ref[stage][owner, pl.ds(first, 1), :],
                            ref[stage][owner, pl.ds(first + 8, 1), :],
                        ],
                        1,
                    )
                    layer = jnp.where(row16 == at, line * valid[slot][face], layer)
                layers.append(layer)
            result.append(own + jnp.concatenate(layers, 0))
        return result

    for stage in range(2):
        resid = local_part(real, imag)
        forward_faces(stage)
        forward_layers(stage)
        if stage:
            sent_all(stage - 1)
        resid_real, resid_imag = add_ghosts(stage, *resid)
        real, imag = (
            real + (resid_real * step_real - resid_imag * step_imag),
            imag + (resid_real * step_imag + resid_imag * step_real),
        )
        put_sheets(stage + 1, real, imag)
        send_layers(stage + 1)
        put_faces(stage + 1, real, imag)
        send_faces(stage + 1)

    resid = local_part(real, imag)
    forward_faces(2)
    forward_layers(2)
    sent_all(1)
    sent_slab(*meta_exchange)
    sent_across(*meta_exchange)
    receive_slab(*meta_exchange)
    receive_across(*meta_exchange)
    gathered = n_sub * 8
    meta_row = iota((gathered, 128), 0)
    meta_lane = iota((gathered, 128), 1)
    selectors = []
    coarse = []
    lane = iota((patch_rows, 128), 1)
    patch = iota((patch_rows, 128), 0)
    sign = jnp.where(lane < 64, -1.0, 1.0)

    def placed_of(selector, values):
        terms = jnp.concatenate(terms_of(values, 3), 1)
        product = jnp.dot(selector, terms, preferred_element_type=F32)
        return product[:, :128] + product[:, 128:256] + product[:, 256:]

    for slab in range(3):
        known = meta[slab].reshape(gathered, 128)
        names = pltpu.roll(known, gathered - slots, 0)
        chosen = ((meta_row & 7) < slots) & (names == (meta_lane + 1).astype(F32))
        selector = chosen.astype(F32).T[:patch_rows].astype(BF16)
        selectors.append(selector)
        coarse_wave = placed_of(selector, known)
        diag = 6.0 / 16.0 - coarse_wave
        side = shift_imag * coarse_wave
        factor = omega_coarse / (diag * diag + side * side)
        coarse.append((coarse_wave, diag * factor, side * factor * sign))

    lane512 = iota((512, 128), 1)
    restrict = block_match(iota((512, 128), 0), lane512)
    grow = block_match(iota((128, 512), 1), iota((128, 512), 0))
    fine_lane = iota((fine_rows, 128), 1)
    same_x = ((iota((fine_rows, 128), 0) & 15) >> 2) == ((fine_lane >> 4) & 3)

    resid_real, resid_imag = add_ghosts(2, *resid)
    sums = times_selector(jnp.concatenate([resid_real, resid_imag], 1), restrict)
    sums = jnp.where(same_x, sums, 0.0) * (1.0 / 64.0)
    lines = [
        jnp.sum(sums[slot * 16 : slot * 16 + 16], axis=0, keepdims=True) for slot in range(slots)
    ]
    lines.append(jnp.zeros((8 - slots, 128), F32))
    rows[1, s] = jnp.concatenate(lines, 0)
    send_across(*coarse_exchange)
    send_slab(*coarse_exchange)

    sent_all(2)
    sent_slab(*coarse_exchange)
    sent_across(*coarse_exchange)

    lane_x = (lane >> 4) & 3
    lane_y = (lane >> 2) & 3
    lane_z = lane & 3
    patch_y = patch >> 2
    patch_z = patch & 3
    y_first = patch_y == 0
    y_last = patch_y >= rows_y - 1
    z_first = patch_z == 0
    z_last = patch_z == PZ - 1

    def turned(values, shift):
        return pltpu.roll(values, shift % 128, 1)

    def moved(values, shift):
        return pltpu.roll(values, shift % patch_rows, 0)

    def across(values, shift, outside):
        return jnp.where(outside, 0.0, moved(values, shift))

    def coarse_sum(lower, values, upper):
        x_down = turned(values, 16)
        x_up = turned(values, -16)
        edge = jnp.zeros_like(values) if lower is None else turned(lower, -48)
        total = jnp.where(lane_x == 0, edge, x_down)
        edge = jnp.zeros_like(values) if upper is None else turned(upper, 48)
        total = total + jnp.where(lane_x == 3, edge, x_up)
        total = total + jnp.where(
            lane_y == 0, turned(across(values, PZ, y_first), -12), turned(values, 4)
        )
        total = total + jnp.where(
            lane_y == 3, turned(across(values, -PZ, y_last), 12), turned(values, -4)
        )
        total = total + jnp.where(
            lane_z == 0, turned(across(values, 1, z_first), -3), turned(values, 1)
        )
        return total + jnp.where(
            lane_z == 3, turned(across(values, -1, z_last), 3), turned(values, -1)
        )

    def coarse_step(slab, values):
        _, near, cross = coarse[slab]
        return values * near + turned(values, 64) * cross

    receive_slab(*coarse_exchange)
    receive_across(*coarse_exchange)
    right = [
        placed_of(selectors[slab], rows[slab].reshape(gathered, 128)) for slab in range(3)
    ]
    there = [has_low.astype(F32), None, has_high.astype(F32)]

    def kept(slab, values):
        return values if there[slab] is None else values * there[slab]

    errors = [kept(slab, coarse_step(slab, right[slab])) for slab in range(3)]
    for sweep in range(CITER - 1):
        following = list(errors)
        for slab in (0, 1, 2) if sweep < CITER - 2 else (1,):
            values = errors[slab]
            lower = errors[slab - 1] if slab > 0 else None
            upper = errors[slab + 1] if slab < 2 else None
            coarse_wave = coarse[slab][0]
            applied = (6.0 * values - coarse_sum(lower, values, upper)) * (1.0 / 16.0)
            applied = applied - coarse_wave * (
                values + shift_imag * sign * turned(values, 64)
            )
            following[slab] = kept(
                slab, values + coarse_step(slab, right[slab] - applied)
            )
        errors = following

    placed_e[...] = errors[1]
    grown = []
    for slot in range(slots):
        line = placed_e[pl.ds(jnp.maximum(patch_of[slot], 0), 1), :]
        grown.append(jnp.broadcast_to(line, (16, 128)))
    grown = jnp.where(same_x, jnp.concatenate(grown, 0), 0.0)
    grown = times_selector(grown, grow)
    for slot in range(slots):
        live = patch_of[slot] >= 0
        span = slice(slot * 16, slot * 16 + 16)
        out_ref[slot, 0] = jnp.where(live, real[span] + grown[span, :256], 0.0)
        out_ref[slot, 1] = jnp.where(live, imag[span] + grown[span, 256:], 0.0)


def body(n_grp, n_sub, field, source, patch_of_slot, neighbour, wave_index, wave_table):
    slots = field.shape[0]
    patch_rows = -(-3 * n_sub // 8) * 8
    stages = ROUNDS + 2
    smem = pl.BlockSpec(memory_space=pltpu.SMEM)
    vmem = pl.BlockSpec(memory_space=pltpu.VMEM)
    dma = pltpu.SemaphoreType.DMA((stages, n_sub))
    return pl.pallas_call(
        functools.partial(kernel, n_grp, n_sub),
        out_shape=jax.ShapeDtypeStruct(field.shape, F32),
        in_specs=[smem] * 4 + [pl.BlockSpec(memory_space=pltpu.HBM)] * 2,
        out_specs=vmem,
        scratch_shapes=[pltpu.VMEM(field.shape, F32)] * 2
        + [pltpu.SemaphoreType.DMA((2,))]
        + [pltpu.VMEM((n_sub * slots, 16, 128), F32)] * ROUNDS
        + [pltpu.VMEM((n_sub, 4 * slots, 128), F32)] * (2 * ROUNDS)
        + [
            pltpu.VMEM((ROUNDS, 2, 4 * slots, 128), F32),
            pltpu.VMEM((3, n_sub, 8, 128), F32),
            pltpu.VMEM((3, n_sub, 8, 128), F32),
            pltpu.VMEM((patch_rows, 128), F32),
        ]
        + [dma] * 6,
        compiler_params=pltpu.CompilerParams(
            collective_id=0, has_side_effects=True, vmem_limit_bytes=24 * 1024 * 1024
        ),
    )(
        *(
            pltpu.with_memory_space_constraint(values, pltpu.HBM)
            for values in (patch_of_slot, neighbour, wave_index, wave_table, field, source)
        ),
    )


def solution(mesh):
    return jax.shard_map(
        functools.partial(body, mesh.shape["grp"], mesh.shape["sub"]),
        mesh=mesh,
        in_specs=(
            P(("grp", "sub"), None, None, None),
            P(("grp", "sub"), None, None, None),
            P(("grp", "sub")),
            P(("grp", "sub"), None),
            P(("grp", "sub")),
            P(),
        ),
        out_specs=P(("grp", "sub"), None, None, None),
        check_vma=False,
    )
```

```python
import functools

import jax
import jax.numpy as jnp
from jax import lax
from jax.experimental import pallas as pl
from jax.experimental.pallas import tpu as pltpu
from jax.sharding import PartitionSpec as P

PZ = 4
CITER = 3
ROUNDS = 3

omega_fine = 0.7
omega_coarse = 0.6
shift_imag = 0.5

F32 = jnp.float32
BF16 = jnp.bfloat16
MESH = pl.DeviceIdType.MESH


def iota(shape, axis):
    return lax.broadcasted_iota(jnp.int32, shape, axis)


def terms_of(values, count):
    terms = []
    for _ in range(count - 1):
        term = values.astype(BF16)
        terms.append(term)
        values = values - term.astype(F32)
    terms.append(values.astype(BF16))
    return terms


def times_selector(values, selector, count=2):
    rows = values.shape[0]
    stacked = jnp.concatenate(terms_of(values, count), 0)
    product = jnp.dot(stacked, selector, preferred_element_type=F32)
    total = product[:rows]
    for term in range(1, count):
        total = total + product[term * rows : (term + 1) * rows]
    return total


def face_cells(shape, lane_axis, opposite):
    lane = iota(shape, lane_axis)
    face = lane >> 5
    if opposite:
        face = face ^ 1
    place = lane & 15
    cell = jnp.where(
        face < 2,
        place + jnp.where(face == 1, 240, 0),
        place * 16 + jnp.where(face == 3, 15, 0),
    )
    return (lane >> 4) & 1, cell


def pack_matrix():
    shape = (512, 128)
    part, cell = face_cells(shape, 1, False)
    return (iota(shape, 0) == part * 256 + cell).astype(F32).astype(BF16)


def unpack_matrix():
    shape = (128, 512)
    part, cell = face_cells(shape, 0, True)
    return (iota(shape, 1) == part * 256 + cell).astype(F32).astype(BF16)


def block_match(fine, lane):
    same_part = (fine >> 8) == (lane >> 6)
    same_y = ((fine >> 6) & 3) == ((lane >> 2) & 3)
    same_z = ((fine >> 2) & 3) == (lane & 3)
    return (same_part & same_y & same_z).astype(F32).astype(BF16)


def kernel(
    n_grp,
    n_sub,
    patch_ref,
    link_ref,
    index_ref,
    table_ref,
    field_in,
    source_in,
    out_ref,
    field_ref,
    source_ref,
    input_sem,
    faces_0,
    faces_1,
    faces_2,
    below_0,
    below_1,
    below_2,
    above_0,
    above_1,
    above_2,
    sheets,
    meta,
    rows,
    placed_e,
    slab_send,
    slab_recv,
    low_send,
    low_recv,
    high_send,
    high_recv,
):
    faces = (faces_0, faces_1, faces_2)
    below = (below_0, below_1, below_2)
    above = (above_0, above_1, above_2)
    slots = field_ref.shape[0]
    fine_rows = slots * 16
    patch_total = 3 * n_sub
    rows_y = patch_total // PZ
    patch_rows = -(-patch_total // 8) * 8
    g = lax.axis_index("grp")
    s = lax.axis_index("sub")
    has_low = g > 0
    has_high = g < n_grp - 1

    def beside(step):
        return lax.rem(s + step, n_sub)

    def before(step):
        return lax.rem(s + n_sub - step, n_sub)

    field_copy = pltpu.make_async_copy(field_in, field_ref, input_sem.at[0])
    source_copy = pltpu.make_async_copy(source_in, source_ref, input_sem.at[1])
    field_copy.start()
    source_copy.start()

    barrier = pltpu.get_barrier_semaphore()
    for step in range(1, n_sub):
        pl.semaphore_signal(barrier, inc=1, device_id=(g, beside(step)), device_id_type=MESH)

    @pl.when(has_low)
    def _():
        for step in range(n_sub):
            pl.semaphore_signal(
                barrier, inc=1, device_id=(g - 1, beside(step)), device_id_type=MESH
            )

    @pl.when(has_high)
    def _():
        for step in range(n_sub):
            pl.semaphore_signal(
                barrier, inc=1, device_id=(g + 1, beside(step)), device_id_type=MESH
            )

    def slab_copy(ref_of, stage, step, owner):
        ref = ref_of(owner)
        return pltpu.make_async_remote_copy(
            src_ref=ref,
            dst_ref=ref,
            send_sem=slab_send.at[stage, step],
            recv_sem=slab_recv.at[stage, step],
            device_id=(g, beside(step)),
            device_id_type=MESH,
        )

    def low_copy(src, dst, stage, step):
        return pltpu.make_async_remote_copy(
            src_ref=src,
            dst_ref=dst,
            send_sem=low_send.at[stage, step],
            recv_sem=high_recv.at[stage, step],
            device_id=(g - 1, beside(step)),
            device_id_type=MESH,
        )

    def high_copy(src, dst, stage, step):
        return pltpu.make_async_remote_copy(
            src_ref=src,
            dst_ref=dst,
            send_sem=high_send.at[stage, step],
            recv_sem=low_recv.at[stage, step],
            device_id=(g + 1, beside(step)),
            device_id_type=MESH,
        )

    def face_copy(stage, owner, to, sem):
        ref = faces[stage].at[pl.ds(owner * slots, slots)]
        return pltpu.make_async_remote_copy(
            src_ref=ref,
            dst_ref=ref,
            send_sem=slab_send.at[stage, sem],
            recv_sem=slab_recv.at[stage, sem],
            device_id=(g, to),
            device_id_type=MESH,
        )

    def send_faces(stage):
        for step in range(1, n_sub):
            face_copy(stage, s, beside(step), step).start()

    def receive_faces(stage):
        for step in range(1, n_sub):
            face_copy(stage, before(step), beside(step), step).wait_recv()

    def sent_faces(stage):
        for step in range(1, n_sub):
            face_copy(stage, s, beside(step), step).wait_send()

    def sent_all(stage):
        sent_faces(stage)
        sent_across(*face_exchange(stage))

    def send_slab(stage, slab_of, *_):
        for step in range(1, n_sub):
            slab_copy(slab_of, stage, step, s).start()

    def send_across(stage, slab_of, low_src, low_of, high_src, high_of):
        @pl.when(has_high)
        def _():
            for step in range(n_sub):
                high_copy(high_src, low_of(s), stage, step).start()

        @pl.when(has_low)
        def _():
            for step in range(n_sub):
                low_copy(low_src, high_of(s), stage, step).start()

    def receive_slab(stage, slab_of, *_):
        for step in range(1, n_sub):
            slab_copy(slab_of, stage, step, before(step)).wait_recv()

    def receive_across(stage, slab_of, low_src, low_of, high_src, high_of):
        @pl.when(has_low)
        def _():
            for step in range(n_sub):
                high_copy(high_src, low_of(before(step)), stage, step).wait_recv()

        @pl.when(has_high)
        def _():
            for step in range(n_sub):
                low_copy(low_src, high_of(before(step)), stage, step).wait_recv()

    def sent_slab(stage, slab_of, *_):
        for step in range(1, n_sub):
            slab_copy(slab_of, stage, step, s).wait_send()

    def sent_across(stage, slab_of, low_src, low_of, high_src, high_of):
        @pl.when(has_high)
        def _():
            for step in range(n_sub):
                high_copy(high_src, low_of(s), stage, step).wait_send()

        @pl.when(has_low)
        def _():
            for step in range(n_sub):
                low_copy(low_src, high_of(s), stage, step).wait_send()

    def face_exchange(stage):
        return (
            stage,
            None,
            sheets.at[stage, 0],
            lambda owner: below[stage].at[owner],
            sheets.at[stage, 1],
            lambda owner: above[stage].at[owner],
        )

    def row_exchange(stage, ref):
        mine = ref.at[1, s]
        return (
            stage,
            lambda owner: ref.at[1, owner],
            mine,
            lambda owner: ref.at[0, owner],
            mine,
            lambda owner: ref.at[2, owner],
        )

    meta_exchange = row_exchange(ROUNDS, meta)
    coarse_exchange = row_exchange(ROUNDS + 1, rows)

    @pl.when(jnp.logical_not(has_low))
    def _():
        for layers in below:
            layers[...] = jnp.zeros_like(layers)
        meta[0] = jnp.zeros_like(meta[0])
        rows[0] = jnp.zeros_like(rows[0])

    @pl.when(jnp.logical_not(has_high))
    def _():
        for layers in above:
            layers[...] = jnp.zeros_like(layers)
        meta[2] = jnp.zeros_like(meta[2])
        rows[2] = jnp.zeros_like(rows[2])

    wave_of = [table_ref[index_ref[slot]] for slot in range(slots)]
    patch_of = [patch_ref[slot] for slot in range(slots)]

    row8 = iota((8, 128), 0)
    meta_rows = jnp.zeros((8, 128), F32)
    for slot in range(slots):
        meta_rows = jnp.where(row8 == slot, wave_of[slot], meta_rows)
        meta_rows = jnp.where(
            row8 == slots + slot, (patch_of[slot] + 1).astype(F32), meta_rows
        )
    meta[1, s] = meta_rows

    def joined(ref, part):
        return jnp.concatenate([ref[slot, part] for slot in range(slots)], 0)

    pack = pack_matrix()
    field_copy.wait()
    real = joined(field_ref, 0)
    imag = joined(field_ref, 1)

    def put_sheets(stage, real, imag):
        for side, edge_row in ((0, 0), (1, 15)):
            lines = []
            for half in range(2):
                for slot in range(slots):
                    for values in (real, imag):
                        row = slot * 16 + edge_row
                        lines.append(values[row : row + 1, half * 128 : half * 128 + 128])
            sheets[stage, side] = jnp.concatenate(lines, 0)

    def put_faces(stage, real, imag):
        packed = times_selector(jnp.concatenate([real, imag], 1), pack)
        for slot in range(slots):
            faces[stage][s * slots + slot] = packed[slot * 16 : slot * 16 + 16]

    put_sheets(0, real, imag)
    put_faces(0, real, imag)

    greeted = n_sub - 1 + n_sub * (has_low.astype(jnp.int32) + has_high.astype(jnp.int32))
    pl.semaphore_wait(barrier, greeted)

    send_faces(0)
    send_across(*face_exchange(0))
    send_slab(*meta_exchange)
    send_across(*meta_exchange)

    source_copy.wait()
    source_real = joined(source_ref, 0)
    source_imag = joined(source_ref, 1)
    unpack = unpack_matrix()
    wave = jnp.concatenate([jnp.full((16, 256), wave_of[slot], F32) for slot in range(slots)], 0)
    real_diag = 6.0 - wave
    imag_diag = shift_imag * wave
    scale = omega_fine / (real_diag * real_diag + imag_diag * imag_diag)
    step_real = real_diag * scale
    step_imag = imag_diag * scale

    cell = iota((fine_rows, 256), 1)
    fine_i = iota((fine_rows, 256), 0) & 15
    y_low = cell < 16
    y_high = cell >= 240
    z_low = (cell & 15) == 0
    z_high = (cell & 15) == 15
    x_low = fine_i == 0
    x_high = fine_i == 15

    def inner_sum(values):
        total = jnp.where(y_low, 0.0, pltpu.roll(values, 16, 1))
        total = total + jnp.where(y_high, 0.0, pltpu.roll(values, 240, 1))
        total = total + jnp.where(z_low, 0.0, pltpu.roll(values, 1, 1))
        total = total + jnp.where(z_high, 0.0, pltpu.roll(values, 255, 1))
        total = total + jnp.where(x_low, 0.0, pltpu.roll(values, 1, 0))
        return total + jnp.where(x_high, 0.0, pltpu.roll(values, fine_rows - 1, 0))

    def local_part(real, imag):
        out_real = (
            source_real
            + inner_sum(real)
            - (6.0 * real - wave * (real - shift_imag * imag))
        )
        out_imag = (
            source_imag
            + inner_sum(imag)
            - (6.0 * imag - wave * (imag + shift_imag * real))
        )
        return out_real, out_imag

    links = [[link_ref[slot, face] for face in range(6)] for slot in range(slots)]
    safe = [[jnp.maximum(link, 0) for link in line] for line in links]
    valid = [[(link >= 0).astype(F32) for link in line] for line in links]
    packed_lane = iota((16, 128), 1) >> 5
    row16 = iota((16, 256), 0)

    def add_ghosts(stage, out_real, out_imag):
        receive_faces(stage)
        blocks = []
        for slot in range(slots):
            got = [
                faces[stage][safe[slot][face]] * valid[slot][face] for face in range(2, 6)
            ]
            blocks.append(
                jnp.where(
                    packed_lane == 1,
                    got[0],
                    jnp.where(
                        packed_lane == 0,
                        got[1],
                        jnp.where(packed_lane == 3, got[2], got[3]),
                    ),
                )
            )
        spread = times_selector(jnp.concatenate(blocks, 0), unpack)
        out_real = out_real + spread[:, :256]
        out_imag = out_imag + spread[:, 256:]
        receive_across(*face_exchange(stage))
        result = []
        for part, own in ((0, out_real), (1, out_imag)):
            layers = []
            for slot in range(slots):
                layer = jnp.zeros((16, 256), F32)
                for face, ref, at in ((0, below, 0), (1, above, 15)):
                    link = safe[slot][face]
                    owner = link >> 2
                    first = (link & 3) * 2 + part
                    line = jnp.concatenate(
                        [
                            ref[stage][owner, pl.ds(first, 1), :],
                            ref[stage][owner, pl.ds(first + 8, 1), :],
                        ],
                        1,
                    )
                    layer = jnp.where(row16 == at, line * valid[slot][face], layer)
                layers.append(layer)
            result.append(own + jnp.concatenate(layers, 0))
        return result

    for stage in range(2):
        resid = local_part(real, imag)
        if stage:
            sent_all(stage - 1)
        resid_real, resid_imag = add_ghosts(stage, *resid)
        real, imag = (
            real + (resid_real * step_real - resid_imag * step_imag),
            imag + (resid_real * step_imag + resid_imag * step_real),
        )
        put_sheets(stage + 1, real, imag)
        send_across(*face_exchange(stage + 1))
        put_faces(stage + 1, real, imag)
        send_faces(stage + 1)

    resid = local_part(real, imag)
    sent_all(1)
    sent_slab(*meta_exchange)
    sent_across(*meta_exchange)
    receive_slab(*meta_exchange)
    receive_across(*meta_exchange)
    gathered = n_sub * 8
    meta_row = iota((gathered, 128), 0)
    meta_lane = iota((gathered, 128), 1)
    selectors = []
    coarse = []
    lane = iota((patch_rows, 128), 1)
    patch = iota((patch_rows, 128), 0)
    sign = jnp.where(lane < 64, -1.0, 1.0)

    def placed_of(selector, values):
        terms = jnp.concatenate(terms_of(values, 3), 1)
        product = jnp.dot(selector, terms, preferred_element_type=F32)
        return product[:, :128] + product[:, 128:256] + product[:, 256:]

    for slab in range(3):
        known = meta[slab].reshape(gathered, 128)
        names = pltpu.roll(known, gathered - slots, 0)
        chosen = ((meta_row & 7) < slots) & (names == (meta_lane + 1).astype(F32))
        selector = chosen.astype(F32).T[:patch_rows].astype(BF16)
        selectors.append(selector)
        coarse_wave = placed_of(selector, known)
        diag = 6.0 / 16.0 - coarse_wave
        side = shift_imag * coarse_wave
        factor = omega_coarse / (diag * diag + side * side)
        coarse.append((coarse_wave, diag * factor, side * factor * sign))

    lane512 = iota((512, 128), 1)
    restrict = block_match(iota((512, 128), 0), lane512)
    grow = block_match(iota((128, 512), 1), iota((128, 512), 0))
    fine_lane = iota((fine_rows, 128), 1)
    same_x = ((iota((fine_rows, 128), 0) & 15) >> 2) == ((fine_lane >> 4) & 3)

    resid_real, resid_imag = add_ghosts(2, *resid)
    sums = times_selector(jnp.concatenate([resid_real, resid_imag], 1), restrict)
    sums = jnp.where(same_x, sums, 0.0) * (1.0 / 64.0)
    lines = [
        jnp.sum(sums[slot * 16 : slot * 16 + 16], axis=0, keepdims=True) for slot in range(slots)
    ]
    lines.append(jnp.zeros((8 - slots, 128), F32))
    rows[1, s] = jnp.concatenate(lines, 0)
    send_across(*coarse_exchange)
    send_slab(*coarse_exchange)

    sent_all(2)
    sent_slab(*coarse_exchange)
    sent_across(*coarse_exchange)

    lane_x = (lane >> 4) & 3
    lane_y = (lane >> 2) & 3
    lane_z = lane & 3
    patch_y = patch >> 2
    patch_z = patch & 3
    y_first = patch_y == 0
    y_last = patch_y >= rows_y - 1
    z_first = patch_z == 0
    z_last = patch_z == PZ - 1

    def turned(values, shift):
        return pltpu.roll(values, shift % 128, 1)

    def moved(values, shift):
        return pltpu.roll(values, shift % patch_rows, 0)

    def across(values, shift, outside):
        return jnp.where(outside, 0.0, moved(values, shift))

    def coarse_sum(lower, values, upper):
        x_down = turned(values, 16)
        x_up = turned(values, -16)
        edge = jnp.zeros_like(values) if lower is None else turned(lower, -48)
        total = jnp.where(lane_x == 0, edge, x_down)
        edge = jnp.zeros_like(values) if upper is None else turned(upper, 48)
        total = total + jnp.where(lane_x == 3, edge, x_up)
        total = total + jnp.where(
            lane_y == 0, turned(across(values, PZ, y_first), -12), turned(values, 4)
        )
        total = total + jnp.where(
            lane_y == 3, turned(across(values, -PZ, y_last), 12), turned(values, -4)
        )
        total = total + jnp.where(
            lane_z == 0, turned(across(values, 1, z_first), -3), turned(values, 1)
        )
        return total + jnp.where(
            lane_z == 3, turned(across(values, -1, z_last), 3), turned(values, -1)
        )

    def coarse_step(slab, values):
        _, near, cross = coarse[slab]
        return values * near + turned(values, 64) * cross

    receive_slab(*coarse_exchange)
    receive_across(*coarse_exchange)
    right = [
        placed_of(selectors[slab], rows[slab].reshape(gathered, 128)) for slab in range(3)
    ]
    there = [has_low.astype(F32), None, has_high.astype(F32)]

    def kept(slab, values):
        return values if there[slab] is None else values * there[slab]

    errors = [kept(slab, coarse_step(slab, right[slab])) for slab in range(3)]
    for sweep in range(CITER - 1):
        following = list(errors)
        for slab in (0, 1, 2) if sweep < CITER - 2 else (1,):
            values = errors[slab]
            lower = errors[slab - 1] if slab > 0 else None
            upper = errors[slab + 1] if slab < 2 else None
            coarse_wave = coarse[slab][0]
            applied = (6.0 * values - coarse_sum(lower, values, upper)) * (1.0 / 16.0)
            applied = applied - coarse_wave * (
                values + shift_imag * sign * turned(values, 64)
            )
            following[slab] = kept(
                slab, values + coarse_step(slab, right[slab] - applied)
            )
        errors = following

    placed_e[...] = errors[1]
    grown = []
    for slot in range(slots):
        line = placed_e[pl.ds(jnp.maximum(patch_of[slot], 0), 1), :]
        grown.append(jnp.broadcast_to(line, (16, 128)))
    grown = jnp.where(same_x, jnp.concatenate(grown, 0), 0.0)
    grown = times_selector(grown, grow)
    for slot in range(slots):
        live = patch_of[slot] >= 0
        span = slice(slot * 16, slot * 16 + 16)
        out_ref[slot, 0] = jnp.where(live, real[span] + grown[span, :256], 0.0)
        out_ref[slot, 1] = jnp.where(live, imag[span] + grown[span, 256:], 0.0)


def body(n_grp, n_sub, field, source, patch_of_slot, neighbour, wave_index, wave_table):
    slots = field.shape[0]
    patch_rows = -(-3 * n_sub // 8) * 8
    stages = ROUNDS + 2
    smem = pl.BlockSpec(memory_space=pltpu.SMEM)
    vmem = pl.BlockSpec(memory_space=pltpu.VMEM)
    dma = pltpu.SemaphoreType.DMA((stages, n_sub))
    return pl.pallas_call(
        functools.partial(kernel, n_grp, n_sub),
        out_shape=jax.ShapeDtypeStruct(field.shape, F32),
        in_specs=[smem] * 4 + [pl.BlockSpec(memory_space=pltpu.HBM)] * 2,
        out_specs=vmem,
        scratch_shapes=[pltpu.VMEM(field.shape, F32)] * 2
        + [pltpu.SemaphoreType.DMA((2,))]
        + [pltpu.VMEM((n_sub * slots, 16, 128), F32)] * ROUNDS
        + [pltpu.VMEM((n_sub, 4 * slots, 128), F32)] * (2 * ROUNDS)
        + [
            pltpu.VMEM((ROUNDS, 2, 4 * slots, 128), F32),
            pltpu.VMEM((3, n_sub, 8, 128), F32),
            pltpu.VMEM((3, n_sub, 8, 128), F32),
            pltpu.VMEM((patch_rows, 128), F32),
        ]
        + [dma] * 6,
        compiler_params=pltpu.CompilerParams(
            collective_id=0, has_side_effects=True, vmem_limit_bytes=24 * 1024 * 1024
        ),
    )(
        *(
            pltpu.with_memory_space_constraint(values, pltpu.HBM)
            for values in (patch_of_slot, neighbour, wave_index, wave_table, field, source)
        ),
    )


def solution(mesh):
    return jax.shard_map(
        functools.partial(body, mesh.shape["grp"], mesh.shape["sub"]),
        mesh=mesh,
        in_specs=(
            P(("grp", "sub"), None, None, None),
            P(("grp", "sub"), None, None, None),
            P(("grp", "sub")),
            P(("grp", "sub"), None),
            P(("grp", "sub")),
            P(),
        ),
        out_specs=P(("grp", "sub"), None, None, None),
        check_vma=False,
    )
```
